256 devices in a mesh: item: 2 (over core), row: 16 (over z, y_hi), col: 8 (over x, y_lo).
Axes of the slice: x: 4, y: 4 (y_hi: 2, y_lo: 2; y = y_hi * 2 + y_lo), z: 8, core: 2. Of those that a mesh axis runs over, the one named last changes fastest.
Arguments:
- hidden_video: bfloat16 [2, 4, 32, 32, 3072], P('item', None, 'row', 'col'), may hold values from -6 to 6
- hidden_text: bfloat16 [2, 226, 3072], P('item'), may hold values from -6 to 6
- step: int32 [2], replicated, may hold values from 0 to 999
- valid_count: int32 [2], replicated, may hold values from 2048 to 4096, as said below
- mod_weight: bfloat16 [6, 512, 3072], P(None, None, ('item', 'row', 'col')), may hold values from -0.25 to 0.25
- query_weight: bfloat16 [3072, 3072], P(('item', 'row'), 'col'), may hold values from -0.109375 to 0.109375
- key_weight: bfloat16 [3072, 3072], P(('item', 'row'), 'col'), may hold values from -0.109375 to 0.109375
- value_weight: bfloat16 [3072, 3072], P(('item', 'row'), 'col'), may hold values from -0.109375 to 0.109375
- out_weight: bfloat16 [3072, 3072], P(('item', 'row'), 'col'), may hold values from -0.109375 to 0.109375
- query_gain: float32 [64], replicated, may hold values from 1 to 6
- key_gain: float32 [64], replicated, may hold values from 1 to 6
Outputs:
- video_out: bfloat16 [2, 4, 32, 32, 3072], P('item', None, 'row', 'col')
The draws below stay inside these ranges and needn't reach their ends.
Inputs may be any that keep to these rules, and one draw needn't show every extreme that they name: The first valid_count[i] video tokens of item i in frame-major order are real; in every draw one item is whole and the other is cut to some length.
All inputs are finite; a program needn't handle non-finite values.
Results may differ from the reference program's by a relative error of at most 0.017.
Values may be sent and summed in bfloat16 or wider, within the bound.
No kernel may reach another device: no remote copies, remote signals or barrier semaphores. Data moves between devices by JAX's collectives and lax.ppermute only.
A program may use at most 128 MiB of HBM per device.

```python
import math
import jax
import jax.numpy as jnp
from jax import lax

D = 3072
HEADS = 48
HDIM = 64
TEMB = 512
TXT = 226
FRAMES = 4
ITEMS = 2
GRID_H = 32
GRID_W = 32
VID = 4096
HD = 3072


def draw_valid_count(key, part):
    short_key, pick_key = jax.random.split(jax.random.fold_in(key, 7))
    shorter = jax.random.randint(short_key, (), VID // 2, VID + 1)
    whole_item = jax.random.randint(pick_key, (), 0, ITEMS)
    return jnp.where(jnp.arange(ITEMS) == whole_item, VID, shorter).astype(jnp.int32)


def gain_law(key):
    return jnp.exp(jax.random.uniform(key, (HDIM,), jnp.float32, 0.0, jnp.log(4.0)))


def draw_query_gain(key, part):
    return gain_law(jax.random.fold_in(key, 11))


def draw_key_gain(key, part):
    return gain_law(jax.random.fold_in(key, 12))


def block_levels(key, shape, cuts, low, largest):
    loudness, own = 1.0, jax.random.fold_in(key, 6)
    for axis_at, shards_of in cuts:
        heights = jnp.exp(jax.random.uniform(jax.random.fold_in(own, axis_at), (shards_of,), jnp.float32, low / len(cuts), largest / len(cuts)))
        loudness = loudness * jnp.repeat(heights, shape[axis_at] // shards_of).reshape([-1 if axis == axis_at else 1 for axis in range(len(shape))])
    return loudness


def scatter_about(own_key, extent, scale, reach, pieces=(), held_as=jnp.bfloat16):
    factor_of = block_levels(own_key, extent, pieces, -0.22, 0.18) if pieces else 1.0
    entries = jax.random.normal(own_key, extent, jnp.float32) * scale * factor_of
    return jnp.minimum(jnp.maximum(entries, -reach), reach).astype(held_as)


def setup_inputs(seed: int = 0) -> dict:
    arg_keys = jax.random.split(jax.random.key(seed), 12)
    return {
        "hidden_video": scatter_about(arg_keys[0], (ITEMS, FRAMES, GRID_H, GRID_W, D), 1.0, 6.0, ((0, 2), (2, 16), (3, 8))),
        "hidden_text": scatter_about(arg_keys[1], (ITEMS, TXT, D), 1.0, 6.0, ((0, 2),)),
        "step": jax.random.randint(arg_keys[2], (ITEMS,), 0, 1000).astype(jnp.int32),
        "valid_count": draw_valid_count(jax.random.fold_in(arg_keys[11], 71), 0),
        "mod_weight": scatter_about(arg_keys[4], (6, TEMB, D), TEMB ** -0.5, 0.25, ((2, 256),)),
        "query_weight": scatter_about(arg_keys[5], (D, HD), D ** -0.5, 0.109375, ((0, 32), (1, 8))),
        "key_weight": scatter_about(arg_keys[6], (D, HD), D ** -0.5, 0.109375, ((0, 32), (1, 8))),
        "value_weight": scatter_about(arg_keys[7], (D, HD), D ** -0.5, 0.109375, ((0, 32), (1, 8))),
        "out_weight": scatter_about(arg_keys[8], (D, HD), HD ** -0.5, 0.109375, ((0, 32), (1, 8))),
        "query_gain": draw_query_gain(jax.random.fold_in(arg_keys[11], 71), 0),
        "key_gain": draw_key_gain(jax.random.fold_in(arg_keys[11], 71), 0),
    }


def layer_norm(values, epsilon):
    center = values - lax.optimization_barrier(jnp.mean(values, axis=-1, keepdims=True))
    spread = lax.optimization_barrier(jnp.mean(center * center, axis=-1, keepdims=True))
    return center * lax.rsqrt(spread + epsilon)

def time_features(steps_in, embed_width):
    half_width = embed_width // 2
    rates = jnp.exp(-math.log(10000.0) * jnp.arange(half_width, dtype=jnp.float32) / half_width)
    phases = steps_in.astype(jnp.float32)[:, None] * rates[None, :]
    return jnp.concatenate([jnp.cos(phases), jnp.sin(phases)], axis=1)

def band_angles(position, band_size):
    half_size = band_size // 2
    rates = jnp.exp(-math.log(10000.0) * (2.0 * jnp.arange(half_size, dtype=jnp.float32) / band_size))
    return position[:, None] * rates[None, :]

def rotary_angles(frame, height, across):
    return jnp.concatenate([band_angles(frame.astype(jnp.float32), 16), band_angles(height.astype(jnp.float32), 24), band_angles(across.astype(jnp.float32), 24)], axis=1)

def rotate(values, angles):
    outputs = []
    offset = 0
    angle_offset = 0
    for band_size in (16, 24, 24):
        half_size = band_size // 2
        front = values[:, :, offset:offset + half_size]
        back = values[:, :, offset + half_size:offset + band_size]
        phase = angles[:, None, angle_offset:angle_offset + half_size]
        cosine = jnp.cos(phase)
        sine = jnp.sin(phase)
        outputs.append(front * cosine - back * sine)
        outputs.append(back * cosine + front * sine)
        offset += band_size
        angle_offset += half_size
    return jnp.concatenate(outputs, axis=-1)

def head_norm(projected, gains):
    row_count = projected.shape[0]
    shaped = projected.reshape(row_count, projected.shape[1] // 64, 64)
    return layer_norm(shaped, 1e-06) * gains

def attend(query, keys, values, usable):

    def one_head(operands):
        query_head, key_head, value_head = operands
        scores = jnp.dot(query_head, key_head.T, preferred_element_type=jnp.float32) * 0.125
        scores = jnp.where(usable[None, :], scores, -jnp.inf)
        best = lax.optimization_barrier(jnp.max(scores, axis=1, keepdims=True))
        powers = jnp.exp(scores - best)
        totals = lax.optimization_barrier(jnp.sum(powers, axis=1, keepdims=True))
        mixed = jnp.dot(powers.astype(jnp.bfloat16), value_head, preferred_element_type=jnp.float32)
        return (mixed / totals).astype(jnp.bfloat16)
    stacked = lax.map(one_head, (jnp.transpose(query, (1, 0, 2)), jnp.transpose(keys, (1, 0, 2)), jnp.transpose(values, (1, 0, 2))))
    return jnp.transpose(stacked, (1, 0, 2))

def reference(hidden_video, hidden_text, step, valid_count, mod_weight, query_weight, key_weight, value_weight, out_weight, query_gain, key_gain):
    features = time_features(step, TEMB)
    active = jax.nn.silu(features).astype(jnp.bfloat16)
    modulation = jnp.einsum('it,jtd->ijd', active.astype(jnp.float32), mod_weight.astype(jnp.float32))
    token_index = jnp.arange(VID, dtype=jnp.int32)
    frame = token_index // (GRID_H * GRID_W)
    height = token_index // GRID_W % GRID_H
    across = token_index % GRID_W
    angles = rotary_angles(frame, height, across)
    results = []
    for item_index in range(ITEMS):
        own_mod = modulation[item_index]
        video_rows = hidden_video[item_index].reshape(VID, D).astype(jnp.float32)
        video_norm = (layer_norm(video_rows, 1e-05) * (1.0 + own_mod[1]) + own_mod[0]).astype(jnp.bfloat16)
        text_rows = hidden_text[item_index].astype(jnp.float32)
        text_norm = (layer_norm(text_rows, 1e-05) * (1.0 + own_mod[4]) + own_mod[3]).astype(jnp.bfloat16)
        query_raw = jnp.dot(video_norm, query_weight, preferred_element_type=jnp.float32)
        key_raw = jnp.dot(video_norm, key_weight, preferred_element_type=jnp.float32)
        value_raw = jnp.dot(video_norm, value_weight, preferred_element_type=jnp.float32)
        text_key_raw = jnp.dot(text_norm, key_weight, preferred_element_type=jnp.float32)
        text_value_raw = jnp.dot(text_norm, value_weight, preferred_element_type=jnp.float32)
        query = rotate(head_norm(query_raw, query_gain), angles).astype(jnp.bfloat16)
        video_key = rotate(head_norm(key_raw, key_gain), angles).astype(jnp.bfloat16)
        text_key = head_norm(text_key_raw, key_gain).astype(jnp.bfloat16)
        video_value = value_raw.astype(jnp.bfloat16).reshape(VID, HEADS, 64)
        text_value = text_value_raw.astype(jnp.bfloat16).reshape(TXT, HEADS, 64)
        keys = jnp.concatenate([text_key, video_key], axis=0)
        values = jnp.concatenate([text_value, video_value], axis=0)
        usable = jnp.concatenate([jnp.ones((TXT,), dtype=bool), token_index < valid_count[item_index]])
        attended = attend(query, keys, values, usable).reshape(VID, HD)
        projected = jnp.dot(attended, out_weight.T, preferred_element_type=jnp.float32)
        video_out = (video_rows + own_mod[2] * projected).astype(jnp.bfloat16)
        results.append(video_out.reshape(FRAMES, GRID_H, GRID_W, D))
    return jnp.stack(results, axis=0)
```

```python
import math

import jax
import jax.numpy as jnp
import numpy as np
from jax import lax
from jax.experimental import pallas as pl
from jax.experimental.pallas import tpu as pltpu
from jax.sharding import PartitionSpec as P

AXES = ("item", "row", "col")
NEG_FILL = -1e30
WIDTH = 3072
BLOCK = 96
TILE = 32
STRIP = 256
VIDEO = 512
TEXT_PART = 32
KEYS = VIDEO + TEXT_PART
ZS = 8
BIG = 60 * 1024 * 1024


def place_of(device):
    c, row, col = device // 128, device // 8 % 16, device % 8
    return c, row // 2, row % 2, col // 2, col % 2


def device_of(c, z, yh, x, yl):
    return c % 2 * 128 + (z % 8 * 2 + yh % 2) * 8 + x % 4 * 2 + yl % 2


def send(values, dc=0, dz=0, dyh=0, dx=0, dyl=0):
    pairs = []
    for device in range(256):
        c, z, yh, x, yl = place_of(device)
        pairs.append((device, device_of(c + dc, z + dz, yh + dyh, x + dx, yl + dyl)))
    return lax.ppermute(values, AXES, pairs)


def trade_items(values):
    pairs = []
    for device in range(256):
        c, z, yh, x, yl = place_of(device)
        pairs.append((device, device_of(yh, z, c, x, yl)))
    return lax.ppermute(values, AXES, pairs)


def call(body, outs, *args, scratch=(), smem=1, flops=0, moved=0):
    specs = [pl.BlockSpec(memory_space=pltpu.SMEM)] * smem
    specs += [pl.BlockSpec(memory_space=pltpu.VMEM)] * (len(args) - smem)
    many = isinstance(outs, (list, tuple))
    out_specs = pl.BlockSpec(memory_space=pltpu.VMEM)
    return pl.pallas_call(
        body,
        out_shape=outs,
        in_specs=specs,
        out_specs=[out_specs] * len(outs) if many else out_specs,
        scratch_shapes=list(scratch),
        compiler_params=pltpu.CompilerParams(vmem_limit_bytes=BIG),
        cost_estimate=pl.CostEstimate(flops=flops, bytes_accessed=moved, transcendentals=0),
    )(*args)


def shape(dims, dtype=jnp.bfloat16):
    return jax.ShapeDtypeStruct(dims, dtype)


def matmul(left, right):
    return jnp.dot(left, right, preferred_element_type=jnp.float32)


def matmul_nt(left, right):
    return lax.dot_general(
        left, right, (((1,), (1,)), ((), ())), preferred_element_type=jnp.float32
    )


def split_weights(ids, key_ref, value_ref, query_ref, out_ref, own_ref, other_ref):
    first = ids[0] == 0
    for at, ref in enumerate((key_ref, value_ref, query_ref, out_ref)):
        full = ref[...].astype(jnp.float32)
        low, high = full[:, :192], full[:, 192:]
        own_ref[:, at * 192 : at * 192 + 192] = jnp.where(first, low, high).astype(jnp.bfloat16)
        other_ref[:, at * 192 : at * 192 + 192] = jnp.where(first, high, low).astype(jnp.bfloat16)


def sort_weights(ids, *refs):
    pieces, (project_ref, out_ref) = refs[:9], refs[9:]
    c, z, yh = ids[0], ids[1], ids[2]
    away = (0, -1, 1, -2, 2, -3, 3, -4, 4)
    for piece, dz in zip(pieces, away):
        if dz == -4:
            parts = (0, 1)
        elif dz == 4:
            parts = (2, 3)
        else:
            parts = (0, 1, 2, 3)
        for at, part in enumerate(parts):
            source_row = (z + dz + ZS) % ZS * 2 + (yh + part // 2) % 2
            source_core = (c + part % 2) % 2
            start = pl.multiple_of((source_core * 16 + source_row) * BLOCK, 32)
            rows = slice(at * BLOCK, at * BLOCK + BLOCK)
            project_ref[pl.ds(start, BLOCK), :] = piece[rows, :640]
            out_ref[pl.ds(start, BLOCK), :] = piece[rows, 512:]


def ring(block, half):
    right, left = [send(block, dz=1)], [send(block, dz=-1)]
    for _ in range(2):
        right.append(send(right[-1], dz=1))
        left.append(send(left[-1], dz=-1))
    right.append(send(right[-1][:half], dz=1))
    left.append(send(left[-1][half:], dz=-1))
    return right, left


def time_features(steps_in, embed_width):
    half_width = embed_width // 2
    rates = jnp.exp(-math.log(10000.0) * jnp.arange(half_width, dtype=jnp.float32) / half_width)
    phases = steps_in.astype(jnp.float32)[:, None] * rates[None, :]
    return jnp.concatenate([jnp.cos(phases), jnp.sin(phases)], axis=1)


def own_modulation(active_ref, weight_ref, slots_ref, tile_ref):
    tile_ref[...] = jnp.zeros_like(tile_ref)
    for part in range(6):
        both = matmul_nt(active_ref[...], weight_ref[part])
        for item in range(2):
            at = item * 8 + part
            tile_ref[at : at + 1, :12] = both[item : item + 1, :]
    for peer in range(8):
        slots_ref[peer] = tile_ref[...]


def join_cols(slots_ref, joined_ref, tile_ref):
    tile_ref[...] = jnp.zeros_like(tile_ref)
    tile_ref[:, :96] = jnp.concatenate([slots_ref[peer][:, :12] for peer in range(8)], axis=1)
    for row in range(16):
        item = row % 2
        joined_ref[row] = tile_ref[item * 8 : item * 8 + 8, :]


def join_rows(ids, own_ref, other_ref, mod_ref):
    own = jnp.concatenate([own_ref[row][:, :96] for row in range(16)], axis=1)
    other = jnp.concatenate([other_ref[row][:, :96] for row in range(16)], axis=1)
    first = ids[0] == 0
    mod_ref[:, : WIDTH // 2] = jnp.where(first, own, other)
    mod_ref[:, WIDTH // 2 :] = jnp.where(first, other, own)


def sort_tiles(ids, near_ref, right_ref, left_ref, far_right_ref, far_left_ref, out_ref):
    x, yl = ids[3], ids[4]
    for ref, dx, parts in (
        (near_ref, 0, (0, 1)),
        (right_ref, -1, (0, 1)),
        (left_ref, 1, (0, 1)),
        (far_right_ref, -2, (0,)),
        (far_left_ref, 2, (1,)),
    ):
        for at, part in enumerate(parts):
            col = (x + dx + 4) % 4 * 2 + (yl + part) % 2
            start = pl.multiple_of(col * TILE, TILE)
            out_ref[pl.ds(start, TILE), :] = ref[at * TILE : at * TILE + TILE, :]


def layer_norm(values, epsilon):
    center = values - jnp.mean(values, axis=-1, keepdims=True)
    spread = jnp.mean(center * center, axis=-1, keepdims=True)
    return center * lax.rsqrt(spread + epsilon)


def split_dot(values, constant):
    high = values.astype(jnp.bfloat16)
    low = (values - high.astype(jnp.float32)).astype(jnp.bfloat16)
    return matmul(high, constant) + matmul(low, constant)


def norm_and_rotate(raw, gain, average, partner, cosine, sine):
    center = raw - split_dot(raw, average)
    spread = split_dot(center * center, average)
    normed = center * lax.rsqrt(spread + 1e-06) * gain
    return normed * cosine + split_dot(normed, partner) * sine


def project(
    ids,
    own_ref,
    other_ref,
    text_ref,
    mod_ref,
    weight_ref,
    average_ref,
    partner_ref,
    cosine_ref,
    sine_ref,
    gain_ref,
    query_out,
    keys_out,
    norm_ref,
):
    c = ids[0]
    shift, scale = mod_ref[0:1, :], 1.0 + mod_ref[1:2, :]
    for ref, core in ((own_ref, c), (other_ref, 1 - c)):

        def some_rows(step, _, ref=ref, core=core):
            at = pl.multiple_of(step * 32, 32)
            rows = ref[pl.ds(at, 32), :].astype(jnp.float32)
            start = pl.multiple_of(core * STRIP + at, 32)
            norm_ref[pl.ds(start, 32), :] = (layer_norm(rows, 1e-05) * scale + shift).astype(
                jnp.bfloat16
            )
            return 0

        lax.fori_loop(0, STRIP // 32, some_rows, 0)
    text = text_ref[...].astype(jnp.float32)
    norm_ref[VIDEO:, :] = (
        layer_norm(text, 1e-05) * (1.0 + mod_ref[4:5, :]) + mod_ref[3:4, :]
    ).astype(jnp.bfloat16)
    lanes = lax.broadcasted_iota(jnp.int32, (1, 256), 1)
    average, partner = average_ref[...], partner_ref[...]
    weight = weight_ref[...]
    for start, size in ((0, 256), (256, 256), (512, 32)):
        rows = slice(start, start + size)
        raw = matmul(norm_ref[rows, :], weight)
        cosine, sine = cosine_ref[rows, :], sine_ref[rows, :]
        key_raw = raw[:, :256]
        key = norm_and_rotate(key_raw, gain_ref[1:2, :], average, partner, cosine, sine)
        keys_out[rows, :256] = jnp.where(lanes < 192, key, key_raw).astype(jnp.bfloat16)
        keys_out[rows, 256:] = raw[:, 256:384].astype(jnp.bfloat16)
        if start < VIDEO:
            query = norm_and_rotate(
                raw[:, 384:640], gain_ref[0:1, :], average, partner, cosine, sine
            )
            query_out[rows, :] = jnp.where(
                lanes < 192, query.astype(jnp.bfloat16).astype(jnp.float32) * 0.125, 0.0
            ).astype(jnp.bfloat16)


def usable_bias(count, first, z, limit):
    token = lax.broadcasted_iota(jnp.int32, (count, 128), 0) + first
    height = 4 * z + token // 256 * 2 + token % 8 // 4
    index = (token % 32 // 8 * 32 + height) * 32 + token % 256 // 32 * 4 + token % 4
    video_ok = jnp.logical_and(token < VIDEO, index < limit)
    text_at = jnp.minimum(TEXT_PART * z, 226 - TEXT_PART) + token - VIDEO
    text_ok = jnp.logical_and(token >= VIDEO, text_at >= TEXT_PART * z)
    return jnp.where(jnp.logical_or(video_ok, text_ok), 0.0, NEG_FILL).astype(jnp.bfloat16)


def attend_pieces(ids, query_ref, pieces, old, new, finish):
    z, limit = ids[1], ids[5]
    loaded = []
    for ref, dz, first, count in pieces:
        values = ref[...]
        bias = usable_bias(count, first, (z + dz + ZS) % ZS, limit)
        loaded.append((values, bias))
    values = jnp.concatenate([entry[0] for entry in loaded], axis=0)
    bias = jnp.concatenate([entry[1] for entry in loaded], axis=0)
    ones = jnp.ones(bias.shape, jnp.bfloat16)
    lanes = lax.broadcasted_iota(jnp.int32, (1, 128), 1)
    pick = jnp.where(lanes == 0, 1.0, 0.0).astype(jnp.bfloat16)
    keys = [jnp.concatenate([values[:, at : at + 128], bias], axis=1) for at in (0, 128)]
    mixes = [jnp.concatenate([values[:, at : at + 128], ones], axis=1) for at in (128, 256)]
    for start in range(0, VIDEO, STRIP):
        rows = slice(start, start + STRIP)
        finished = []
        for head in range(3):
            key_tile, mix_tile = (0, 0, 1)[head], (0, 1, 1)[head]
            inside = (lanes < 64) if head != 1 else (lanes >= 64)
            query = query_ref[rows, key_tile * 128 : key_tile * 128 + 128]
            query = jnp.where(inside, query, jnp.zeros_like(query))
            query = jnp.concatenate([query, jnp.broadcast_to(pick, query.shape)], axis=1)
            scores = matmul_nt(query, keys[key_tile])
            best = jnp.max(scores, axis=1, keepdims=True)
            if old is None:
                powers = jnp.exp(scores - best).astype(jnp.bfloat16)
                mixed = matmul(powers, mixes[mix_tile])
                gathered, total = mixed[:, :128], mixed[:, 128:]
                best = jnp.broadcast_to(best, gathered.shape)
            else:
                best_old = old[0][head, rows, :]
                best = jnp.maximum(best_old, best)
                powers = jnp.exp(scores - best[:, :1]).astype(jnp.bfloat16)
                mixed = matmul(powers, mixes[mix_tile])
                rescale = jnp.exp(best_old - best)
                total = old[1][head, rows, :] * rescale + mixed[:, 128:]
                gathered = old[2][head, rows, :] * rescale + mixed[:, :128]
            if finish is None:
                new[0][head, rows, :] = best
                new[1][head, rows, :] = total
                new[2][head, rows, :] = gathered
            else:
                finished.append(gathered / total)
        if finish is not None:
            attended_ref = finish
            attended_ref[rows, :128] = jnp.where(lanes < 64, 0.0, finished[0]).astype(jnp.bfloat16)
            attended_ref[rows, 128:] = jnp.where(lanes < 64, finished[1], finished[2]).astype(
                jnp.bfloat16
            )


def attend_first(ids, query_ref, own_ref, *new):
    attend_pieces(ids, query_ref, [(own_ref, 0, 0, KEYS)], None, new, None)


def attend_more(dz, ids, query_ref, right_ref, left_ref, *states):
    pieces = [(right_ref, -dz, 0, KEYS), (left_ref, dz, 0, KEYS)]
    attend_pieces(ids, query_ref, pieces, states[:3], states[3:], None)


def attend_last(
    ids, query_ref, right_ref, left_ref, best, total, gathered, weight_ref, own_out, send_out, done
):
    half = KEYS // 2
    pieces = [(right_ref, -4, 0, half), (left_ref, 4, half, half)]
    attend_pieces(ids, query_ref, pieces, (best, total, gathered), None, done)
    c = ids[0]
    own_at = pl.multiple_of(c * STRIP, STRIP)
    other_at = pl.multiple_of((1 - c) * STRIP, STRIP)
    weight = weight_ref[...]
    send_out[...] = matmul_nt(done[pl.ds(other_at, STRIP), :], weight).astype(jnp.bfloat16)
    own_out[...] = matmul_nt(done[pl.ds(own_at, STRIP), :], weight).astype(jnp.bfloat16)


def add_two(left_ref, right_ref, out_ref):
    out_ref[...] = (
        left_ref[...].astype(jnp.float32) + right_ref[...].astype(jnp.float32)
    ).astype(jnp.bfloat16)


def finish_rows(parts_ref, hidden_ref, mod_ref, out_ref):
    total = parts_ref[0:TILE, :].astype(jnp.float32)
    for peer in range(1, 8):
        total += parts_ref[peer * TILE : peer * TILE + TILE, :].astype(jnp.float32)
    out_ref[...] = (hidden_ref[...].astype(jnp.float32) + mod_ref[2:3, :] * total).astype(
        jnp.bfloat16
    )


def band_angles(position, band_size):
    half_size = band_size // 2
    rates = jnp.exp(
        -math.log(10000.0) * (2.0 * jnp.arange(half_size, dtype=jnp.float32) / band_size)
    )
    return position[:, None] * rates[None, :]


def rotary_tables(z):
    token = jnp.arange(VIDEO, dtype=jnp.int32)
    frame = token % 32 // 8
    height = 4 * z + token // 256 * 2 + token % 8 // 4
    across = token % 256 // 32 * 4 + token % 4
    cosines, sines = [], []
    for place, band in ((frame, 16), (height, 24), (across, 24)):
        angles = band_angles(place.astype(jnp.float32), band)
        cosine, sine = jnp.cos(angles), jnp.sin(angles)
        cosines += [cosine, cosine]
        sines += [-sine, sine]
    cosine = jnp.tile(jnp.concatenate(cosines, axis=1), (1, 4))
    sine = jnp.tile(jnp.concatenate(sines, axis=1), (1, 4))
    return (
        jnp.pad(cosine, ((0, TEXT_PART), (0, 0)), constant_values=1.0),
        jnp.pad(sine, ((0, TEXT_PART), (0, 0))),
    )


def constant_matrices():
    average = np.zeros((256, 256), np.float32)
    partner = np.zeros((256, 256), np.float32)
    for head in range(4):
        average[head * 64 : head * 64 + 64, head * 64 : head * 64 + 64] = 1.0 / 64
        at = head * 64
        for band in (16, 24, 24):
            half = band // 2
            for entry in range(half):
                partner[at + half + entry, at + entry] = 1.0
                partner[at + entry, at + half + entry] = 1.0
            at += band
    return jnp.asarray(average, jnp.bfloat16), jnp.asarray(partner, jnp.bfloat16)


def on_device(
    hidden_video,
    hidden_text,
    step,
    valid_count,
    mod_weight,
    query_weight,
    key_weight,
    value_weight,
    out_weight,
    query_gain,
    key_gain,
):
    c = lax.axis_index("item")
    row = lax.axis_index("row")
    col = lax.axis_index("col")
    z, yh = row // 2, row % 2
    limit = lax.dynamic_index_in_dim(valid_count, yh, 0, keepdims=False)
    ids = jnp.stack([c, z, yh, col // 2, col % 2, limit]).astype(jnp.int32)

    with jax.named_scope("weights"):
        own, other = call(
            split_weights,
            [shape((BLOCK, 768))] * 2,
            ids,
            key_weight,
            value_weight,
            query_weight,
            out_weight,
        )
        pair = jnp.concatenate([own, send(other, dc=1)], axis=0)
        block = jnp.concatenate([pair, send(pair, dyh=1)], axis=0)
        right, left = ring(block, 2 * BLOCK)
        project_weight, last_weight = call(
            sort_weights,
            [shape((WIDTH, 640)), shape((WIDTH, 256))],
            ids,
            block,
            right[0],
            left[0],
            right[1],
            left[1],
            right[2],
            left[2],
            right[3],
            left[3],
            moved=4 << 20,
        )

    with jax.named_scope("tokens"):
        tile = trade_items(hidden_video.reshape(TILE, WIDTH))
        near = jnp.concatenate([tile, send(tile, dyl=1)], axis=0)
        from_right, from_left = send(near, dx=1), send(near, dx=-1)
        far_right, far_left = send(from_right[:TILE], dx=1), send(from_left[TILE:], dx=-1)
        strip = call(
            sort_tiles,
            shape((STRIP, WIDTH)),
            ids,
            near,
            from_right,
            from_left,
            far_right,
            far_left,
        )
        other_strip = send(strip, dc=1)
        text_own = lax.dynamic_slice_in_dim(
            hidden_text[0], jnp.minimum(TEXT_PART * z, 226 - TEXT_PART), TEXT_PART, 0
        )
        text = jnp.where(c == yh, text_own, send(text_own, dc=1))

    with jax.named_scope("modulation"):
        active = jax.nn.silu(time_features(step, 512)).astype(jnp.bfloat16)
        slots = call(
            own_modulation,
            shape((8, 16, 128), jnp.float32),
            active,
            jnp.transpose(mod_weight, (0, 2, 1)),
            scratch=[pltpu.VMEM((16, 128), jnp.float32)],
            smem=0,
        )
        slots = lax.all_to_all(slots, "col", 0, 0, tiled=True)
        joined = call(
            join_cols,
            shape((16, 8, 128), jnp.float32),
            slots,
            scratch=[pltpu.VMEM((16, 128), jnp.float32)],
            smem=0,
        )
        joined = lax.all_to_all(joined, "row", 0, 0, tiled=True)
        modulation = call(
            join_rows, shape((8, WIDTH), jnp.float32), ids, joined, send(joined, dc=1)
        )

    with jax.named_scope("projections"):
        average, partner = constant_matrices()
        cosine, sine = rotary_tables(z)
        gains = jnp.tile(jnp.stack([query_gain, key_gain]), (1, 4))
        query, keys = call(
            project,
            [shape((VIDEO, 256)), shape((KEYS, 384))],
            ids,
            strip,
            other_strip,
            text,
            modulation,
            project_weight,
            average,
            partner,
            cosine,
            sine,
            gains,
            scratch=[pltpu.VMEM((KEYS, WIDTH), jnp.bfloat16)],
            flops=2 * KEYS * WIDTH * 640,
        )

    with jax.named_scope("attention"):
        right, left = ring(keys, KEYS // 2)
        state_shapes = [shape((3, VIDEO, 128), jnp.float32)] * 3
        cost = 4 * VIDEO * KEYS * 256 * 3
        state = call(attend_first, state_shapes, ids, query, keys, flops=cost)
        for away in range(1, 4):

            def more(*refs, away=away):
                attend_more(away, *refs)

            state = call(
                more,
                state_shapes,
                ids,
                query,
                right[away - 1],
                left[away - 1],
                *state,
                flops=2 * cost,
            )
        own_rows, other_rows = call(
            attend_last,
            [shape((STRIP, WIDTH))] * 2,
            ids,
            query,
            right[3],
            left[3],
            *state,
            last_weight,
            scratch=[pltpu.VMEM((VIDEO, 256), jnp.bfloat16)],
            flops=cost,
        )

    with jax.named_scope("output"):
        summed = call(
            add_two, shape((STRIP, WIDTH)), own_rows, send(other_rows, dc=1), smem=0
        )
        parts = lax.all_to_all(summed, "col", 0, 0, tiled=True)
        result = call(
            finish_rows, shape((TILE, WIDTH)), parts, tile, modulation, smem=0
        )
        return trade_items(result).reshape(hidden_video.shape)


def solution(mesh):
    placed = (
        P("item", None, "row", "col", None),
        P("item", None, None),
        P(),
        P(),
        P(None, None, ("item", "row", "col")),
        P(("item", "row"), "col"),
        P(("item", "row"), "col"),
        P(("item", "row"), "col"),
        P(("item", "row"), "col"),
        P(),
        P(),
    )
    return jax.shard_map(
        on_device,
        mesh=mesh,
        in_specs=placed,
        out_specs=P("item", None, "row", "col", None),
        check_vma=False,
    )
```

```python
import math

import jax
import jax.numpy as jnp
import numpy as np
from jax import lax
from jax.experimental import pallas as pl
from jax.experimental.pallas import tpu as pltpu
from jax.sharding import PartitionSpec as P

AXES = ("item", "row", "col")
NEG_FILL = -1e30
WIDTH = 3072
BLOCK = 96
TILE = 32
STRIP = 256
VIDEO = 512
TEXT_PART = 32
KEYS = VIDEO + TEXT_PART
ZS = 8


def place_of(device):
    c, row, col = device // 128, device // 8 % 16, device % 8
    return c, row // 2, row % 2, col // 2, col % 2


def device_of(c, z, yh, x, yl):
    return c % 2 * 128 + (z % 8 * 2 + yh % 2) * 8 + x % 4 * 2 + yl % 2


def send(values, dc=0, dz=0, dyh=0, dx=0, dyl=0):
    pairs = []
    for device in range(256):
        c, z, yh, x, yl = place_of(device)
        pairs.append((device, device_of(c + dc, z + dz, yh + dyh, x + dx, yl + dyl)))
    return lax.ppermute(values, AXES, pairs)


def trade_items(values, other=0):
    pairs = []
    for device in range(256):
        c, z, yh, x, yl = place_of(device)
        pairs.append((device, device_of(yh, z, c + other, x, yl)))
    return lax.ppermute(values, AXES, pairs)


def call(body, outs, *args, scratch=(), smem=1, flops=0, moved=0, room=12):
    specs = [pl.BlockSpec(memory_space=pltpu.SMEM)] * smem
    specs += [pl.BlockSpec(memory_space=pltpu.VMEM)] * (len(args) - smem)
    many = isinstance(outs, (list, tuple))
    out_specs = pl.BlockSpec(memory_space=pltpu.VMEM)
    return pl.pallas_call(
        body,
        out_shape=outs,
        in_specs=specs,
        out_specs=[out_specs] * len(outs) if many else out_specs,
        scratch_shapes=list(scratch),
        compiler_params=pltpu.CompilerParams(vmem_limit_bytes=room << 20),
        cost_estimate=pl.CostEstimate(flops=flops, bytes_accessed=moved, transcendentals=0),
    )(*args)


def shape(dims, dtype=jnp.bfloat16):
    return jax.ShapeDtypeStruct(dims, dtype)


def matmul(left, right):
    return jnp.dot(left, right, preferred_element_type=jnp.float32)


def matmul_nt(left, right):
    return lax.dot_general(
        left, right, (((1,), (1,)), ((), ())), preferred_element_type=jnp.float32
    )


MODS, KEYS_AT, QUERY_AT, OUT_AT, BLOCK_ROWS, CUT = 16, 16, 400, 496, 592, 304


def heads_of(values, first):
    values = values.astype(jnp.float32)
    return jnp.where(first, values[:, :192], values[:, 192:])


def stack_weights(key_ref, value_ref, out_ref):
    out_ref[:BLOCK, :] = key_ref[...]
    out_ref[BLOCK:, :] = value_ref[...]


def split_weights(ids, near_ref, far_ref, query_ref, other_ref):
    second = ids[0] != 0
    for ref, yh in ((near_ref, ids[2]), (far_ref, 1 - ids[2])):
        rows = pl.ds(pl.multiple_of(yh * BLOCK, 32), BLOCK)
        parts = [heads_of(ref[at * BLOCK : at * BLOCK + BLOCK, :], second) for at in range(2)]
        other_ref[rows, :] = jnp.concatenate(parts, axis=1).astype(jnp.bfloat16)
    query = heads_of(query_ref[...], second)
    other_ref[2 * BLOCK :, :] = jnp.concatenate([query, query], axis=1).astype(jnp.bfloat16)


def join_weights(
    ids, near_ref, far_ref, other_ref, query_ref, out_ref, own_mod, pair_mod, block_ref
):
    c, yh = ids[0], ids[2]
    first = c == 0
    for ref, at in ((near_ref, yh), (far_ref, 1 - yh)):
        at = pl.multiple_of(at * BLOCK, 32)
        parts = [heads_of(ref[at * BLOCK : at * BLOCK + BLOCK, :], first) for at in range(2)]
        start = pl.multiple_of(KEYS_AT + c * 192 + at, 16)
        block_ref[pl.ds(start, BLOCK), :] = jnp.concatenate(parts, axis=1).astype(jnp.bfloat16)
        start = pl.multiple_of(KEYS_AT + (1 - c) * 192 + at, 16)
        block_ref[pl.ds(start, BLOCK), :] = other_ref[pl.ds(at, BLOCK), :]
    query = heads_of(query_ref[...], first)
    other = other_ref[2 * BLOCK :, :].astype(jnp.float32)[:, :192]
    low, high = jnp.where(first, query, other), jnp.where(first, other, query)
    block_ref[QUERY_AT:OUT_AT, :] = jnp.concatenate([low, high], axis=1).astype(jnp.bfloat16)
    block_ref[OUT_AT:, :] = out_ref[...]
    item = pl.ds(pl.multiple_of(yh * 8, 8), 8)
    mods = {}
    for ref, half in ((own_mod, 0), (pair_mod, 1)):
        mine, others = ref[0, item, :][:, :96], ref[1, item, :][:, :96]
        mods[half] = (jnp.where(first, mine, others), jnp.where(first, others, mine))
    own_first = yh == 0
    lanes = []
    for core in range(2):
        own, other = mods[0][core], mods[1][core]
        lanes += [jnp.where(own_first, own, other), jnp.where(own_first, other, own)]
    full = jnp.concatenate(lanes, axis=1)
    high = full.astype(jnp.bfloat16).astype(jnp.float32)
    middle = (full - high).astype(jnp.bfloat16).astype(jnp.float32)
    low = full - high - middle
    rows = [term[part : part + 1, :] for term in (high, middle, low) for part in range(5)]
    rows.append(jnp.zeros_like(rows[0]))
    block_ref[:MODS, :] = jnp.concatenate(rows, axis=0).astype(jnp.bfloat16)


AWAY = (0, -1, 1, -2, 2, -3, 3)


def sort_later(ids, *refs):
    z = ids[1]
    pieces, (query_out, out_out) = refs[:8], refs[8:]
    for ref, dz in zip(pieces, AWAY + (4,)):
        at = ref.shape[0] - 2 * BLOCK
        rows = pl.ds(pl.multiple_of((z + dz + ZS) % ZS * BLOCK, 32), BLOCK)
        query_out[rows, :] = ref[at : at + BLOCK, :]
        out_out[rows, :] = ref[at + BLOCK :, :]


def sort_out(ids, near_ref, far_ref, weight_ref):
    for ref, yh in ((near_ref, ids[2]), (far_ref, 1 - ids[2])):
        for z in range(ZS):
            rows = pl.ds(pl.multiple_of(z * 192 + yh * BLOCK, 32), BLOCK)
            weight_ref[rows, :] = ref[z * BLOCK : z * BLOCK + BLOCK, :]


def time_features(steps_in, embed_width):
    half_width = embed_width // 2
    rates = jnp.exp(-math.log(10000.0) * jnp.arange(half_width, dtype=jnp.float32) / half_width)
    phases = steps_in.astype(jnp.float32)[:, None] * rates[None, :]
    return jnp.concatenate([jnp.cos(phases), jnp.sin(phases)], axis=1)


def own_modulation(active_ref, weight_ref, slots_ref, tile_ref):
    tile_ref[...] = jnp.zeros_like(tile_ref)
    for part in range(6):
        both = matmul_nt(active_ref[...], weight_ref[part])
        for item in range(2):
            at = item * 8 + part
            tile_ref[at : at + 1, :12] = both[item : item + 1, :]
    for peer in range(8):
        slots_ref[peer] = tile_ref[...]


def join_cols(slots_ref, joined_ref):
    joined_ref[...] = jnp.zeros_like(joined_ref)
    joined_ref[:, :96] = jnp.concatenate([slots_ref[peer][:, :12] for peer in range(8)], axis=1)


def sort_tiles(ids, near_ref, right_ref, left_ref, far_right_ref, far_left_ref, out_ref):
    x, yl = ids[3], ids[4]
    for ref, dx, parts in (
        (near_ref, 0, (0, 1)),
        (right_ref, -1, (0, 1)),
        (left_ref, 1, (0, 1)),
        (far_right_ref, -2, (0,)),
        (far_left_ref, 2, (1,)),
    ):
        for at, part in enumerate(parts):
            col = (x + dx + 4) % 4 * 2 + (yl + part) % 2
            start = pl.multiple_of(col * TILE, TILE)
            out_ref[pl.ds(start, TILE), :] = ref[at * TILE : at * TILE + TILE, :]


def layer_norm(values, epsilon):
    center = values - jnp.mean(values, axis=-1, keepdims=True)
    spread = jnp.mean(center * center, axis=-1, keepdims=True)
    return center * lax.rsqrt(spread + epsilon)


def split_dot(values, constant):
    high = values.astype(jnp.bfloat16)
    low = (values - high.astype(jnp.float32)).astype(jnp.bfloat16)
    return matmul(high, constant) + matmul(low, constant)


def norm_and_rotate(raw, gain, average, partner, cosine, sine):
    center = raw - split_dot(raw, average)
    spread = split_dot(center * center, average)
    normed = center * lax.rsqrt(spread + 1e-06) * gain
    return normed * cosine + split_dot(normed, partner) * sine


def norm_tokens(ids, own_ref, other_ref, text_ref, norm_ref):
    c = ids[0]
    for ref, start, count in (
        (own_ref, c * STRIP, STRIP),
        (other_ref, (1 - c) * STRIP, STRIP),
        (text_ref, VIDEO, TEXT_PART),
    ):

        def step(at, _, ref=ref, start=start):
            at = pl.multiple_of(at * 16, 16)
            norm_ref[pl.ds(pl.multiple_of(start + at, 16), 16), :] = layer_norm(
                ref[pl.ds(at, 16), :].astype(jnp.float32), 1e-05
            )
            return 0

        lax.fori_loop(0, count // 16, step, 0, unroll=2)


def project_keys(ids, norm_ref, *refs):
    z = ids[1]
    pieces, rest = refs[:9], refs[9:]
    (average_ref, partner_ref, cosine_ref, sine_ref, gain_ref) = rest[:5]
    keys_out, input_out, mod_out, weight_ref, terms_ref = rest[5:]
    places = [(z + dz + ZS) % ZS for dz in AWAY + (4,)]
    for ref, place in zip(pieces[:8], places):
        terms = ref[:MODS, :].astype(jnp.float32)
        terms_ref[place] = jnp.concatenate(
            [terms[:5] + terms[5:10] + terms[10:15], jnp.zeros((3, 384), jnp.float32)], axis=0
        )
    for core in range(2):
        mods = [terms_ref[place][:, core * 192 : core * 192 + 192] for place in range(ZS)]
        mod_out[:, core * 1536 : core * 1536 + 1536] = jnp.concatenate(mods, axis=1)
    for start, count, part in ((0, VIDEO, 0), (VIDEO, TEXT_PART, 3)):
        scale, shift = 1.0 + mod_out[part + 1 : part + 2, :], mod_out[part : part + 1, :]

        def step(at, _, start=start, scale=scale, shift=shift):
            rows = pl.ds(pl.multiple_of(start + at * 16, 16), 16)
            input_out[rows, :] = (norm_ref[rows, :] * scale + shift).astype(jnp.bfloat16)
            return 0

        lax.fori_loop(0, count // 16, step, 0, unroll=2)
    for ref, place in zip(pieces[:7], places):
        for core in range(2):
            start = pl.multiple_of(core * 1536 + place * 192, 32)
            at = KEYS_AT + core * 192
            weight_ref[pl.ds(start, 192), :] = ref[at : at + 192, :]
    right_ref, left_ref, place = pieces[7], pieces[8], places[7]
    start = pl.multiple_of(place * 192, 32)
    weight_ref[pl.ds(start, 192), :] = right_ref[KEYS_AT : KEYS_AT + 192, :]
    start = pl.multiple_of(1536 + place * 192, 32)
    weight_ref[pl.ds(start, BLOCK), :] = right_ref[KEYS_AT + 192 :, :]
    start = pl.multiple_of(1536 + place * 192 + BLOCK, 32)
    weight_ref[pl.ds(start, BLOCK), :] = left_ref[:BLOCK, :]
    raw = matmul(input_out[...], weight_ref[...])
    lanes = lax.broadcasted_iota(jnp.int32, (1, 256), 1)
    key_raw = raw[:, :256]
    key = norm_and_rotate(
        key_raw,
        gain_ref[1:2, :],
        average_ref[...],
        partner_ref[...],
        cosine_ref[...],
        sine_ref[...],
    )
    keys_out[:, :256] = jnp.where(lanes < 192, key, key_raw).astype(jnp.bfloat16)
    keys_out[:, 256:] = raw[:, 256:384].astype(jnp.bfloat16)


def project_query(ids, input_ref, near_ref, far_ref, *refs):
    average_ref, partner_ref, cosine_ref, sine_ref, gain_ref, out, weight_ref = refs
    weight_ref[:, 192:] = jnp.zeros((WIDTH, 64), jnp.bfloat16)
    for ref, yh in ((near_ref, ids[2]), (far_ref, 1 - ids[2])):
        for z in range(ZS):
            values = ref[z * BLOCK : z * BLOCK + BLOCK, :].astype(jnp.float32)
            for core in range(2):
                start = pl.multiple_of(core * 1536 + z * 192 + yh * BLOCK, 32)
                weight_ref[pl.ds(start, BLOCK), :192] = values[
                    :, core * 192 : core * 192 + 192
                ].astype(jnp.bfloat16)
    raw = matmul(input_ref[:VIDEO, :], weight_ref[...])
    query = norm_and_rotate(
        raw,
        gain_ref[0:1, :],
        average_ref[...],
        partner_ref[...],
        cosine_ref[:VIDEO, :],
        sine_ref[:VIDEO, :],
    )
    out[...] = (query.astype(jnp.bfloat16).astype(jnp.float32) * 0.125).astype(jnp.bfloat16)


def rotary_tables(ids, rate_ref, cosine_ref, sine_ref):
    token = lax.broadcasted_iota(jnp.int32, (KEYS, 256), 0)
    lane = lax.broadcasted_iota(jnp.int32, (KEYS, 256), 1) % 64
    frame = token % 32 // 8
    height = 4 * ids[1] + token // 256 * 2 + token % 8 // 4
    across = token % 256 // 32 * 4 + token % 4
    place = jnp.where(lane < 16, frame, jnp.where(lane < 40, height, across))
    angle = jnp.where(token < VIDEO, place.astype(jnp.float32) * rate_ref[...], 0.0)
    back = jnp.logical_or(
        jnp.logical_and(lane >= 8, lane < 16),
        jnp.logical_or(jnp.logical_and(lane >= 28, lane < 40), lane >= 52),
    )
    cosine_ref[...] = jnp.cos(angle)
    sine = jnp.sin(angle)
    sine_ref[...] = jnp.where(back, sine, -sine)


def usable_bias(count, first, z, limit):
    token = lax.broadcasted_iota(jnp.int32, (count, 128), 0) + first
    height = 4 * z + token // 256 * 2 + token % 8 // 4
    index = (token % 32 // 8 * 32 + height) * 32 + token % 256 // 32 * 4 + token % 4
    video_ok = jnp.logical_and(token < VIDEO, index < limit)
    text_at = jnp.minimum(TEXT_PART * z, 226 - TEXT_PART) + token - VIDEO
    text_ok = jnp.logical_and(token >= VIDEO, text_at >= TEXT_PART * z)
    return jnp.where(jnp.logical_or(video_ok, text_ok), 0.0, NEG_FILL).astype(jnp.bfloat16)


def attend_pieces(ids, query_ref, pieces, old, new, finish):
    z, limit = ids[1], ids[5]
    loaded = []
    for ref, dz, first, count in pieces:
        values = ref[...]
        bias = usable_bias(count, first, (z + dz + ZS) % ZS, limit)
        loaded.append((values, bias))
    values = jnp.concatenate([entry[0] for entry in loaded], axis=0)
    bias = jnp.concatenate([entry[1] for entry in loaded], axis=0)
    ones = jnp.ones(bias.shape, jnp.bfloat16)
    lanes = lax.broadcasted_iota(jnp.int32, (1, 128), 1)
    pick = jnp.where(lanes == 0, 1.0, 0.0).astype(jnp.bfloat16)
    keys = [jnp.concatenate([values[:, at : at + 128], bias], axis=1) for at in (0, 128)]
    mixes = [jnp.concatenate([values[:, at : at + 128], ones], axis=1) for at in (128, 256)]
    for start in range(0, VIDEO, STRIP):
        rows = slice(start, start + STRIP)
        finished = []
        for head in range(3):
            key_tile, mix_tile = (0, 0, 1)[head], (0, 1, 1)[head]
            inside = (lanes < 64) if head != 1 else (lanes >= 64)
            query = query_ref[rows, key_tile * 128 : key_tile * 128 + 128]
            query = jnp.where(inside, query, jnp.zeros_like(query))
            query = jnp.concatenate([query, jnp.broadcast_to(pick, query.shape)], axis=1)
            scores = matmul_nt(query, keys[key_tile])
            best = jnp.max(scores, axis=1, keepdims=True)
            if old is None:
                powers = jnp.exp(scores - best).astype(jnp.bfloat16)
                mixed = matmul(powers, mixes[mix_tile])
                gathered, total = mixed[:, :128], mixed[:, 128:]
                best = jnp.broadcast_to(best, gathered.shape)
            else:
                best_old = old[0][head, rows, :]
                best = jnp.maximum(best_old, best)
                powers = jnp.exp(scores - best[:, :1]).astype(jnp.bfloat16)
                mixed = matmul(powers, mixes[mix_tile])
                rescale = jnp.exp(best_old - best)
                total = old[1][head, rows, :] * rescale + mixed[:, 128:]
                gathered = old[2][head, rows, :] * rescale + mixed[:, :128]
            if finish is None:
                new[0][head, rows, :] = best
                new[1][head, rows, :] = total
                new[2][head, rows, :] = gathered
            else:
                finished.append(gathered / total)
        if finish is not None:
            finish[rows, :] = jnp.concatenate(
                [finished[0][:, 64:], finished[1][:, :64], finished[2][:, 64:]], axis=1
            ).astype(jnp.bfloat16)


def attend_first(ids, query_ref, own_ref, *new):
    attend_pieces(ids, query_ref, [(own_ref, 0, 0, KEYS)], None, new, None)


def attend_more(dz, ids, query_ref, right_ref, left_ref, *states):
    pieces = [(right_ref, -dz, 0, KEYS), (left_ref, dz, 0, KEYS)]
    attend_pieces(ids, query_ref, pieces, states[:3], states[3:], None)


def attend_last(ids, query_ref, right_ref, left_ref, best, total, gathered, out_ref):
    half = KEYS // 2
    pieces = [(right_ref, -4, 0, half), (left_ref, 4, half, half)]
    attend_pieces(ids, query_ref, pieces, (best, total, gathered), None, out_ref)


def project_out(ids, own_ref, other_ref, weight_ref, out_ref):
    first = ids[0] == 0
    own_row = pl.multiple_of(ids[0] * STRIP, STRIP)
    other_row = pl.multiple_of((1 - ids[0]) * STRIP, STRIP)
    weight = weight_ref[...]
    for at, start in enumerate((own_row, other_row)):
        own = own_ref[pl.ds(start, STRIP), :].astype(jnp.float32)
        other = other_ref[pl.ds(start, STRIP), :].astype(jnp.float32)
        attended = jnp.concatenate(
            [jnp.where(first, own, other), jnp.where(first, other, own)], axis=1
        ).astype(jnp.bfloat16)
        summed = matmul_nt(attended, weight).astype(jnp.bfloat16)
        for col in range(8):
            out_ref[col, at * TILE : at * TILE + TILE, :] = summed[
                col * TILE : col * TILE + TILE, :
            ]


def finish_rows(ids, parts_ref, own_ref, other_ref, mod_ref, home_ref, away_ref):
    half = WIDTH // 2
    lanes = pl.ds(pl.multiple_of(ids[0] * half, half), half)
    rows = pl.ds(pl.multiple_of((ids[3] * 2 + ids[4]) * TILE, TILE), TILE)
    gate = mod_ref[2:3, lanes]
    for at, hidden_ref, out_ref in ((0, own_ref, home_ref), (TILE, other_ref, away_ref)):
        total = parts_ref[0, at : at + TILE, :].astype(jnp.float32)
        for peer in range(1, 8):
            total += parts_ref[peer, at : at + TILE, :].astype(jnp.float32)
        hidden = hidden_ref[rows, lanes].astype(jnp.float32)
        out_ref[...] = (hidden + gate * total).astype(jnp.bfloat16)


def rotary_rates():
    rates = []
    for band in (16, 24, 24):
        half = band // 2
        rate = jnp.exp(-math.log(10000.0) * (2.0 * jnp.arange(half, dtype=jnp.float32) / band))
        rates += [rate, rate]
    return jnp.tile(jnp.concatenate(rates), 4)[None, :]


def constant_matrices():
    average = np.zeros((256, 256), np.float32)
    partner = np.zeros((256, 256), np.float32)
    for head in range(4):
        average[head * 64 : head * 64 + 64, head * 64 : head * 64 + 64] = 1.0 / 64
        at = head * 64
        for band in (16, 24, 24):
            half = band // 2
            for entry in range(half):
                partner[at + half + entry, at + entry] = 1.0
                partner[at + entry, at + half + entry] = 1.0
            at += band
    return jnp.asarray(average, jnp.bfloat16), jnp.asarray(partner, jnp.bfloat16)


def on_device(
    hidden_video,
    hidden_text,
    step,
    valid_count,
    mod_weight,
    query_weight,
    key_weight,
    value_weight,
    out_weight,
    query_gain,
    key_gain,
):
    c = lax.axis_index("item")
    row = lax.axis_index("row")
    col = lax.axis_index("col")
    z, yh = row // 2, row % 2
    limit = lax.dynamic_index_in_dim(valid_count, yh, 0, keepdims=False)
    ids = jnp.stack([c, z, yh, col // 2, col % 2, limit]).astype(jnp.int32)

    after = lax.optimization_barrier
    with jax.named_scope("start"):
        near_rows = call(stack_weights, shape((2 * BLOCK, 384)), key_weight, value_weight, smem=0)
        far_rows = send(near_rows, dyh=1)
        active = jax.nn.silu(time_features(step, 512)).astype(jnp.bfloat16)
        slots = call(
            own_modulation,
            shape((8, 16, 128), jnp.float32),
            active,
            jnp.transpose(mod_weight, (0, 2, 1)),
            scratch=[pltpu.VMEM((16, 128), jnp.float32)],
            smem=0,
        )
        slots = lax.all_to_all(slots, "col", 0, 0, tiled=True)
        tile = trade_items(hidden_video.reshape(TILE, WIDTH))
        far_rows, slots, tile = after((far_rows, slots, tile))

    with jax.named_scope("block"):
        mod = call(join_cols, shape((16, 128), jnp.float32), slots, smem=0)
        other = call(
            split_weights, shape((3 * BLOCK, 384)), ids, near_rows, far_rows, query_weight
        )
        mods = jnp.stack([mod, send(mod, dc=1)])
        far_mods = send(mods, dyh=1)
        next_tile = send(tile, dyl=1)
        block = call(
            join_weights,
            shape((BLOCK_ROWS, 384)),
            ids,
            near_rows,
            far_rows,
            send(other, dc=1),
            query_weight,
            out_weight,
            mods,
            far_mods,
        )
        block, next_tile = after((block, next_tile))

    with jax.named_scope("ring1"):
        right, left = send(block, dz=1), send(block, dz=-1)
        near = jnp.concatenate([tile, next_tile], axis=0)
        near_right, near_left = send(near, dx=1), send(near, dx=-1)
        text = lax.dynamic_slice_in_dim(
            hidden_text[0], jnp.minimum(TEXT_PART * z, 226 - TEXT_PART), TEXT_PART, 0
        )
        average, partner = constant_matrices()
        cosine, sine = call(
            rotary_tables, [shape((KEYS, 256), jnp.float32)] * 2, ids, rotary_rates()
        )
        gains = jnp.tile(jnp.stack([query_gain, key_gain]), (1, 4))
        tables = (average, partner, cosine, sine, gains)
        right, left, near_right, near_left, text, tables = after(
            (right, left, near_right, near_left, text, tables)
        )
    pieces = [block, right, left]

    with jax.named_scope("ring2"):
        right, left = send(right, dz=1), send(left, dz=-1)
        far_right, far_left = send(near_right[:TILE], dx=1), send(near_left[TILE:], dx=-1)
        text_other = send(text, dc=1)
        strip = call(
            sort_tiles,
            shape((STRIP, WIDTH)),
            ids,
            near,
            near_right,
            near_left,
            far_right,
            far_left,
            room=16,
        )
        right, left, strip, text_other = after((right, left, strip, text_other))
    pieces += [right, left]

    with jax.named_scope("ring3"):
        right, left = send(right, dz=1), send(left, dz=-1)
        other_strip = send(strip, dc=1)
        text = jnp.where(c == yh, text, text_other)
        right, left, other_strip, text = after((right, left, other_strip, text))
    pieces += [right, left]

    with jax.named_scope("ring4"):
        right = send(right[:CUT], dz=1)
        left = send(left[CUT:], dz=-1)
        normed = call(
            norm_tokens,
            shape((KEYS, WIDTH), jnp.float32),
            ids,
            strip,
            other_strip,
            text,
            room=16,
        )
        right, left, normed = after((right, left, normed))

    with jax.named_scope("projections"):
        keys, inputs, modulation = call(
            project_keys,
            [shape((KEYS, 384)), shape((KEYS, WIDTH)), shape((8, WIDTH), jnp.float32)],
            ids,
            normed,
            *pieces,
            right,
            left,
            *tables,
            scratch=[pltpu.VMEM((WIDTH, 384), jnp.bfloat16), pltpu.VMEM((ZS, 8, 384), jnp.float32)],
            flops=2 * KEYS * WIDTH * 384,
            room=32,
        )
        keys, pieces, left_last = after((keys, pieces, left))

    with jax.named_scope("attention"):
        state_shapes = [shape((3, VIDEO, 128), jnp.float32)] * 3
        cost = 4 * VIDEO * KEYS * 256 * 3
        right, left = send(keys, dz=1), send(keys, dz=-1)
        query_near, out_near = call(
            sort_later, [shape((ZS * BLOCK, 384))] * 2, ids, *pieces, left_last
        )
        query_far = send(query_near, dyh=1)
        right, left, query_far = after((right, left, query_far))
        rights, lefts = [right], [left]
        right, left = send(right, dz=1), send(left, dz=-1)
        out_far = send(out_near, dyh=1)
        query = call(
            project_query,
            shape((VIDEO, 256)),
            ids,
            inputs,
            query_near,
            query_far,
            *tables,
            scratch=[pltpu.VMEM((WIDTH, 256), jnp.bfloat16)],
            flops=2 * VIDEO * WIDTH * 256,
            room=24,
        )
        state = call(attend_first, state_shapes, ids, query, keys, flops=cost)
        right, left, *state = after((right, left, *state))

        def more(away, state):
            def body(*refs):
                attend_more(away, *refs)

            args = (ids, query, rights[away - 1], lefts[away - 1], *state)
            return call(body, state_shapes, *args, flops=2 * cost)

        rights.append(right)
        lefts.append(left)
        right, left = send(right, dz=1), send(left, dz=-1)
        state = more(1, state)
        right, left, *state = after((right, left, *state))
        rights.append(right)
        lefts.append(left)
        right, left = send(right[: KEYS // 2], dz=1), send(left[KEYS // 2 :], dz=-1)
        last_weight = call(sort_out, shape((WIDTH // 2, 384)), ids, out_near, out_far)
        state = more(3, more(2, state))
        right, left, last_weight, *state = after((right, left, last_weight, *state))
        attended = call(
            attend_last, shape((VIDEO, 192)), ids, query, right, left, *state, flops=cost
        )

    with jax.named_scope("output"):
        parts = call(
            project_out,
            shape((8, 2 * TILE, WIDTH // 2)),
            ids,
            attended,
            send(attended, dc=1),
            last_weight,
        )
        parts = lax.all_to_all(parts, "col", 0, 0, tiled=True)
        home, away = call(
            finish_rows,
            [shape((TILE, WIDTH // 2))] * 2,
            ids,
            parts,
            strip,
            other_strip,
            modulation,
        )
        home, away = trade_items(home), trade_items(away, other=1)
        low = jnp.where(yh == 0, home, away)
        high = jnp.where(yh == 0, away, home)
        return jnp.concatenate([low, high], axis=1).reshape(hidden_video.shape)


def solution(mesh):
    placed = (
        P("item", None, "row", "col", None),
        P("item", None, None),
        P(),
        P(),
        P(None, None, ("item", "row", "col")),
        P(("item", "row"), "col"),
        P(("item", "row"), "col"),
        P(("item", "row"), "col"),
        P(("item", "row"), "col"),
        P(),
        P(),
    )
    return jax.shard_map(
        on_device,
        mesh=mesh,
        in_specs=placed,
        out_specs=P("item", None, "row", "col", None),
        check_vma=False,
    )
```

```python
import math

import jax
import jax.numpy as jnp
import numpy as np
from jax import lax
from jax.experimental import pallas as pl
from jax.experimental.pallas import tpu as pltpu
from jax.sharding import PartitionSpec as P

AXES = ("item", "row", "col")
NEG_FILL = -1e30
WIDTH = 3072
BLOCK = 96
HALF = 48
TILE = 32
STRIP = 256
VIDEO = 512
TEXT_PART = 32
KEYS = VIDEO + TEXT_PART
ZS = 8


def place_of(device):
    c, row, col = device // 128, device // 8 % 16, device % 8
    return c, row // 2, row % 2, col // 2, col % 2


def device_of(c, z, yh, x, yl):
    return c % 2 * 128 + (z % 8 * 2 + yh % 2) * 8 + x % 4 * 2 + yl % 2


def send(values, dc=0, dz=0, dyh=0, dx=0, dyl=0):
    pairs = []
    for device in range(256):
        c, z, yh, x, yl = place_of(device)
        pairs.append((device, device_of(c + dc, z + dz, yh + dyh, x + dx, yl + dyl)))
    return lax.ppermute(values, AXES, pairs)


def trade_items(values):
    pairs = []
    for device in range(256):
        c, z, yh, x, yl = place_of(device)
        pairs.append((device, device_of(yh, z, c, x, yl)))
    return lax.ppermute(values, AXES, pairs)


def call(body, outs, *args, scratch=(), smem=1, flops=0, moved=0, room=12):
    specs = [pl.BlockSpec(memory_space=pltpu.SMEM)] * smem
    specs += [pl.BlockSpec(memory_space=pltpu.VMEM)] * (len(args) - smem)
    many = isinstance(outs, (list, tuple))
    out_specs = pl.BlockSpec(memory_space=pltpu.VMEM)
    return pl.pallas_call(
        body,
        out_shape=outs,
        in_specs=specs,
        out_specs=[out_specs] * len(outs) if many else out_specs,
        scratch_shapes=list(scratch),
        compiler_params=pltpu.CompilerParams(vmem_limit_bytes=room << 20),
        cost_estimate=pl.CostEstimate(flops=flops, bytes_accessed=moved, transcendentals=0),
    )(*args)


def shape(dims, dtype=jnp.bfloat16):
    return jax.ShapeDtypeStruct(dims, dtype)


def matmul(left, right):
    return jnp.dot(left, right, preferred_element_type=jnp.float32)


def matmul_nt(left, right):
    return lax.dot_general(
        left, right, (((1,), (1,)), ((), ())), preferred_element_type=jnp.float32
    )


MODS, KEYS_AT, QUERY_AT, OUT_AT, BLOCK_ROWS, CUT = 16, 16, 400, 496, 592, 304


def heads_of(values, first):
    values = values.astype(jnp.float32)
    return jnp.where(first, values[:, :192], values[:, 192:])


def stack_rows(first_ref, second_ref, out_ref):
    count = first_ref.shape[0]
    out_ref[:count, :] = first_ref[...]
    out_ref[count:, :] = second_ref[...]


def split_weights(ids, near_ref, far_ref, query_ref, other_ref):
    second = ids[0] != 0
    for ref, yh in ((near_ref, ids[2]), (far_ref, 1 - ids[2])):
        rows = pl.ds(pl.multiple_of(yh * BLOCK, 32), BLOCK)
        parts = [heads_of(ref[at * BLOCK : at * BLOCK + BLOCK, :], second) for at in range(2)]
        other_ref[rows, :] = jnp.concatenate(parts, axis=1).astype(jnp.bfloat16)
    query = heads_of(query_ref[...], second)
    other_ref[2 * BLOCK :, :] = jnp.concatenate([query, query], axis=1).astype(jnp.bfloat16)


def join_weights(
    ids, near_ref, far_ref, other_ref, query_ref, out_ref, slots_ref, block_ref
):
    c, yh = ids[0], ids[2]
    first = c == 0
    for ref, at in ((near_ref, yh), (far_ref, 1 - yh)):
        at = pl.multiple_of(at * BLOCK, 32)
        parts = [heads_of(ref[at * BLOCK : at * BLOCK + BLOCK, :], first) for at in range(2)]
        start = pl.multiple_of(KEYS_AT + c * 192 + at, 16)
        block_ref[pl.ds(start, BLOCK), :] = jnp.concatenate(parts, axis=1).astype(jnp.bfloat16)
        start = pl.multiple_of(KEYS_AT + (1 - c) * 192 + at, 16)
        block_ref[pl.ds(start, BLOCK), :] = other_ref[pl.ds(at, BLOCK), :]
    query = heads_of(query_ref[...], first)
    other = other_ref[2 * BLOCK :, :].astype(jnp.float32)[:, :192]
    low, high = jnp.where(first, query, other), jnp.where(first, other, query)
    block_ref[QUERY_AT:OUT_AT, :] = jnp.concatenate([low, high], axis=1).astype(jnp.bfloat16)
    block_ref[OUT_AT:, :] = out_ref[...]
    full = jnp.concatenate([slots_ref[peer][:, :12] for peer in range(32)], axis=1)
    high = full.astype(jnp.bfloat16).astype(jnp.float32)
    middle = (full - high).astype(jnp.bfloat16).astype(jnp.float32)
    low = full - high - middle
    rows = [term[part : part + 1, :] for term in (high, middle, low) for part in range(5)]
    rows.append(jnp.zeros_like(rows[0]))
    block_ref[:MODS, :] = jnp.concatenate(rows, axis=0).astype(jnp.bfloat16)


AWAY = (0, -1, 1, -2, 2, -3, 3)


def sort_out(ids, near_ref, far_ref, weight_ref):
    for ref, yh in ((near_ref, ids[2]), (far_ref, 1 - ids[2])):
        for z in range(ZS):
            rows = pl.ds(pl.multiple_of(z * 192 + yh * BLOCK, 32), BLOCK)
            weight_ref[rows, :] = ref[z * BLOCK : z * BLOCK + BLOCK, :]


def time_features(steps_in, embed_width):
    half_width = embed_width // 2
    rates = jnp.exp(-math.log(10000.0) * jnp.arange(half_width, dtype=jnp.float32) / half_width)
    phases = steps_in.astype(jnp.float32)[:, None] * rates[None, :]
    return jnp.concatenate([jnp.cos(phases), jnp.sin(phases)], axis=1)


def own_modulation(active_ref, weight_ref, slots_ref, tile_ref):
    tile_ref[...] = jnp.zeros_like(tile_ref)
    for part in range(6):
        both = matmul_nt(active_ref[...], weight_ref[part])
        for item in range(2):
            at = item * 8 + part
            tile_ref[at : at + 1, :12] = both[item : item + 1, :]
    for peer in range(32):
        item = peer // 8 % 2
        slots_ref[peer] = tile_ref[item * 8 : item * 8 + 8, :]


def layer_norm(values, epsilon):
    center = values - jnp.mean(values, axis=-1, keepdims=True)
    spread = jnp.mean(center * center, axis=-1, keepdims=True)
    return center * lax.rsqrt(spread + epsilon)


def split_dot(values, constant):
    high = values.astype(jnp.bfloat16)
    low = (values - high.astype(jnp.float32)).astype(jnp.bfloat16)
    return matmul(high, constant) + matmul(low, constant)


def norm_and_rotate(raw, gain, average, partner, cosine, sine):
    center = raw - split_dot(raw, average)
    spread = split_dot(center * center, average)
    normed = center * lax.rsqrt(spread + 1e-06) * gain
    return normed * cosine + split_dot(normed, partner) * sine


def norm_tokens(*refs):
    start = 0
    for ref in refs[:-1]:

        def step(at, _, ref=ref, start=start):
            at = pl.multiple_of(at * 16, 16)
            refs[-1][pl.ds(pl.multiple_of(start + at, 16), 16), :] = layer_norm(
                ref[pl.ds(at, 16), :].astype(jnp.float32), 1e-05
            )
            return 0

        lax.fori_loop(0, ref.shape[0] // 16, step, 0, unroll=2)
        start += ref.shape[0]


TILES = (
    ((0, 0, 0), (0, 1, 0), (0, 0, 1), (0, 1, 1)),
    (
        (-1, 0, 0),
        (-1, 1, 0),
        (1, 0, 0),
        (1, 1, 0),
        (-1, 0, 1),
        (-1, 1, 1),
        (1, 0, 1),
        (1, 1, 1),
    ),
    ((-2, 0, 0), (2, 1, 0), (-2, 0, 1), (2, 1, 1)),
)


def project_keys(ids, first_ref, second_ref, third_ref, *refs):
    c, z, x, yl = ids[0], ids[1], ids[3], ids[4]
    pieces, rest = refs[:9], refs[9:]
    (average_ref, partner_ref, cosine_ref, sine_ref, gain_ref) = rest[:5]
    keys_out, input_out, low_out, high_out, out_out, mod_ref, weight_ref, terms_ref = rest[5:]
    places = [(z + dz + ZS) % ZS for dz in AWAY + (4,)]
    for ref, place in zip(pieces[:8], places):
        terms = ref[:MODS, :].astype(jnp.float32)
        terms_ref[place] = jnp.concatenate(
            [terms[:5] + terms[5:10] + terms[10:15], jnp.zeros((3, 384), jnp.float32)], axis=0
        )
    for core in range(2):
        mods = [terms_ref[place][:, core * 192 : core * 192 + 192] for place in range(ZS)]
        mod_ref[:, core * 1536 : core * 1536 + 1536] = jnp.concatenate(mods, axis=1)
    for ref, place in zip(pieces[:7] + pieces[8:], places):
        at = ref.shape[0] - 2 * BLOCK
        rows = pl.ds(pl.multiple_of(place * BLOCK, 32), BLOCK)
        out_out[rows, :] = ref[at + BLOCK :, :]
        rows = pl.ds(pl.multiple_of(place * HALF, 16), HALF)
        low_out[rows, :] = ref[at : at + HALF, :]
        high_out[rows, :] = ref[at + HALF : at + BLOCK, :]
    moves = []
    for ref, tiles in zip((first_ref, second_ref, third_ref), TILES):
        for at, (dx, part, core) in enumerate(tiles):
            col = (x + dx + 4) % 4 * 2 + (yl + part) % 2
            moves.append((ref, at * TILE, (c + core) % 2 * STRIP + col * TILE, 0))
    moves.append((third_ref, 4 * TILE, VIDEO, 3))
    for ref, source, target, part in moves:
        scale, shift = 1.0 + mod_ref[part + 1 : part + 2, :], mod_ref[part : part + 1, :]
        for at in (0, 16):
            rows = ref[source + at : source + at + 16, :] * scale + shift
            input_out[pl.ds(pl.multiple_of(target + at, 16), 16), :] = rows.astype(jnp.bfloat16)
    for ref, place in zip(pieces[:7], places):
        for core in range(2):
            start = pl.multiple_of(core * 1536 + place * 192, 32)
            at = KEYS_AT + core * 192
            weight_ref[pl.ds(start, 192), :] = ref[at : at + 192, :]
    right_ref, left_ref, place = pieces[7], pieces[8], places[7]
    start = pl.multiple_of(place * 192, 32)
    weight_ref[pl.ds(start, 192), :] = right_ref[KEYS_AT : KEYS_AT + 192, :]
    start = pl.multiple_of(1536 + place * 192, 32)
    weight_ref[pl.ds(start, BLOCK), :] = right_ref[KEYS_AT + 192 :, :]
    start = pl.multiple_of(1536 + place * 192 + BLOCK, 32)
    weight_ref[pl.ds(start, BLOCK), :] = left_ref[:BLOCK, :]
    raw = matmul(input_out[...], weight_ref[...])
    lanes = lax.broadcasted_iota(jnp.int32, (1, 256), 1)
    key_raw = raw[:, :256]
    key = norm_and_rotate(
        key_raw,
        gain_ref[1:2, :],
        average_ref[...],
        partner_ref[...],
        cosine_ref[...],
        sine_ref[...],
    )
    keys_out[:, :256] = jnp.where(lanes < 192, key, key_raw).astype(jnp.bfloat16)
    keys_out[:, 256:] = raw[:, 256:384].astype(jnp.bfloat16)


def project_query(ids, input_ref, near_low, near_high, far_low, far_high, *refs):
    average_ref, partner_ref, cosine_ref, sine_ref, gain_ref, out, weight_ref = refs
    weight_ref[:, 192:] = jnp.zeros((WIDTH, 64), jnp.bfloat16)
    yh = ids[2]
    for ref, at in (
        (near_low, yh * BLOCK),
        (near_high, yh * BLOCK + HALF),
        (far_low, (1 - yh) * BLOCK),
        (far_high, (1 - yh) * BLOCK + HALF),
    ):
        for z in range(ZS):
            values = ref[z * HALF : z * HALF + HALF, :].astype(jnp.float32)
            for core in range(2):
                start = pl.multiple_of(core * 1536 + z * 192 + at, 16)
                weight_ref[pl.ds(start, HALF), :192] = values[
                    :, core * 192 : core * 192 + 192
                ].astype(jnp.bfloat16)
    raw = matmul(input_ref[:VIDEO, :], weight_ref[...])
    query = norm_and_rotate(
        raw,
        gain_ref[0:1, :],
        average_ref[...],
        partner_ref[...],
        cosine_ref[:VIDEO, :],
        sine_ref[:VIDEO, :],
    )
    out[...] = (query.astype(jnp.bfloat16).astype(jnp.float32) * 0.125).astype(jnp.bfloat16)


def rotary_tables(ids, rate_ref, cosine_ref, sine_ref):
    token = lax.broadcasted_iota(jnp.int32, (KEYS, 256), 0)
    lane = lax.broadcasted_iota(jnp.int32, (KEYS, 256), 1) % 64
    frame = token % 32 // 8
    height = 4 * ids[1] + token // 256 * 2 + token % 8 // 4
    across = token % 256 // 32 * 4 + token % 4
    place = jnp.where(lane < 16, frame, jnp.where(lane < 40, height, across))
    angle = jnp.where(token < VIDEO, place.astype(jnp.float32) * rate_ref[...], 0.0)
    back = jnp.logical_or(
        jnp.logical_and(lane >= 8, lane < 16),
        jnp.logical_or(jnp.logical_and(lane >= 28, lane < 40), lane >= 52),
    )
    cosine_ref[...] = jnp.cos(angle)
    sine = jnp.sin(angle)
    sine_ref[...] = jnp.where(back, sine, -sine)


def usable_bias(count, first, z, limit):
    token = lax.broadcasted_iota(jnp.int32, (count, 128), 0) + first
    height = 4 * z + token // 256 * 2 + token % 8 // 4
    index = (token % 32 // 8 * 32 + height) * 32 + token % 256 // 32 * 4 + token % 4
    video_ok = jnp.logical_and(token < VIDEO, index < limit)
    text_at = jnp.minimum(TEXT_PART * z, 226 - TEXT_PART) + token - VIDEO
    text_ok = jnp.logical_and(token >= VIDEO, text_at >= TEXT_PART * z)
    return jnp.where(jnp.logical_or(video_ok, text_ok), 0.0, NEG_FILL).astype(jnp.bfloat16)


def attend_pieces(ids, counts, query_ref, pieces, old, new, finish):
    z, limit = ids[1], counts[ids[2]]
    loaded = []
    for ref, dz, first, count in pieces:
        values = ref[...]
        bias = usable_bias(count, first, (z + dz + ZS) % ZS, limit)
        loaded.append((values, bias))
    values = jnp.concatenate([entry[0] for entry in loaded], axis=0)
    bias = jnp.concatenate([entry[1] for entry in loaded], axis=0)
    ones = jnp.ones(bias.shape, jnp.bfloat16)
    lanes = lax.broadcasted_iota(jnp.int32, (1, 128), 1)
    pick = jnp.where(lanes == 0, 1.0, 0.0).astype(jnp.bfloat16)
    keys = [jnp.concatenate([values[:, at : at + 128], bias], axis=1) for at in (0, 128)]
    mixes = [jnp.concatenate([values[:, at : at + 128], ones], axis=1) for at in (128, 256)]
    for start in range(0, VIDEO, STRIP):
        rows = slice(start, start + STRIP)
        finished = []
        for head in range(3):
            key_tile, mix_tile = (0, 0, 1)[head], (0, 1, 1)[head]
            inside = (lanes < 64) if head != 1 else (lanes >= 64)
            query = query_ref[rows, key_tile * 128 : key_tile * 128 + 128]
            query = jnp.where(inside, query, jnp.zeros_like(query))
            query = jnp.concatenate([query, jnp.broadcast_to(pick, query.shape)], axis=1)
            scores = matmul_nt(query, keys[key_tile])
            best = jnp.max(scores, axis=1, keepdims=True)
            if old is None:
                powers = jnp.exp(scores - best).astype(jnp.bfloat16)
                mixed = matmul(powers, mixes[mix_tile])
                gathered, total = mixed[:, :128], mixed[:, 128:]
                best = jnp.broadcast_to(best, gathered.shape)
            else:
                best_old = old[0][head, rows, :]
                best = jnp.maximum(best_old, best)
                powers = jnp.exp(scores - best[:, :1]).astype(jnp.bfloat16)
                mixed = matmul(powers, mixes[mix_tile])
                rescale = jnp.exp(best_old - best)
                total = old[1][head, rows, :] * rescale + mixed[:, 128:]
                gathered = old[2][head, rows, :] * rescale + mixed[:, :128]
            if finish is None:
                new[0][head, rows, :] = best
                new[1][head, rows, :] = total
                new[2][head, rows, :] = gathered
            else:
                finished.append(gathered / total)
        if finish is not None:
            finish[rows, :] = jnp.concatenate(
                [finished[0][:, 64:], finished[1][:, :64], finished[2][:, 64:]], axis=1
            ).astype(jnp.bfloat16)


def attend_first(ids, counts, query_ref, own_ref, *new):
    attend_pieces(ids, counts, query_ref, [(own_ref, 0, 0, KEYS)], None, new, None)


def attend_more(dz, ids, counts, query_ref, right_ref, left_ref, *states):
    pieces = [(right_ref, -dz, 0, KEYS), (left_ref, dz, 0, KEYS)]
    attend_pieces(ids, counts, query_ref, pieces, states[:3], states[3:], None)


def attend_last(ids, counts, query_ref, right_ref, left_ref, best, total, gathered, out_ref):
    half = KEYS // 2
    pieces = [(right_ref, -4, 0, half), (left_ref, 4, half, half)]
    attend_pieces(ids, counts, query_ref, pieces, (best, total, gathered), None, out_ref)


def project_out(ids, own_ref, other_ref, weight_ref, mod_ref, out_ref):
    first = ids[0] == 0
    half = WIDTH // 2
    gate = mod_ref[2:3, pl.ds(pl.multiple_of(ids[0] * half, half), half)]
    weight = weight_ref[...]
    for row in range(2):
        rows = slice(row * STRIP, row * STRIP + STRIP)
        own, other = own_ref[rows, :].astype(jnp.float32), other_ref[rows, :].astype(jnp.float32)
        attended = jnp.concatenate(
            [jnp.where(first, own, other), jnp.where(first, other, own)], axis=1
        ).astype(jnp.bfloat16)
        gated = (matmul_nt(attended, weight) * gate).astype(jnp.bfloat16)
        for col in range(8):
            out_ref[row * 8 + col] = gated[col * TILE : col * TILE + TILE, :]


def sum_cols(ids, parts_ref, own_ref, other_ref):
    for ref, item in ((own_ref, ids[0]), (other_ref, 1 - ids[0])):
        total = parts_ref[item * 8].astype(jnp.float32)
        for peer in range(1, 8):
            total += parts_ref[item * 8 + peer].astype(jnp.float32)
        ref[...] = total.astype(ref.dtype)


def finish_rows(ids, hidden_ref, own_ref, other_ref, out_ref):
    first = ids[0] == 0
    half = WIDTH // 2
    own, other = own_ref[...], other_ref[...].astype(jnp.float32)
    low, high = jnp.where(first, own, other), jnp.where(first, other, own)
    out_ref[:, :half] = (hidden_ref[:, :half].astype(jnp.float32) + low).astype(jnp.bfloat16)
    out_ref[:, half:] = (hidden_ref[:, half:].astype(jnp.float32) + high).astype(jnp.bfloat16)


def rotary_rates():
    rates = []
    for band in (16, 24, 24):
        half = band // 2
        rate = jnp.exp(-math.log(10000.0) * (2.0 * jnp.arange(half, dtype=jnp.float32) / band))
        rates += [rate, rate]
    return jnp.tile(jnp.concatenate(rates), 4)[None, :]


def constant_matrices():
    average = np.zeros((256, 256), np.float32)
    partner = np.zeros((256, 256), np.float32)
    for head in range(4):
        average[head * 64 : head * 64 + 64, head * 64 : head * 64 + 64] = 1.0 / 64
        at = head * 64
        for band in (16, 24, 24):
            half = band // 2
            for entry in range(half):
                partner[at + half + entry, at + entry] = 1.0
                partner[at + entry, at + half + entry] = 1.0
            at += band
    return jnp.asarray(average, jnp.bfloat16), jnp.asarray(partner, jnp.bfloat16)


def on_device(
    hidden_video,
    hidden_text,
    step,
    valid_count,
    mod_weight,
    query_weight,
    key_weight,
    value_weight,
    out_weight,
    query_gain,
    key_gain,
):
    c = lax.axis_index("item")
    row = lax.axis_index("row")
    col = lax.axis_index("col")
    z, yh = row // 2, row % 2
    ids = jnp.stack([c, z, yh, col // 2, col % 2]).astype(jnp.int32)
    after = lax.optimization_barrier

    with jax.named_scope("start"):
        near_rows = call(stack_rows, shape((2 * BLOCK, 384)), key_weight, value_weight, smem=0)
        far_rows = send(near_rows, dyh=1)
        home_tile = hidden_video.reshape(TILE, WIDTH)
        tile = trade_items(home_tile)
        active = jax.nn.silu(time_features(step, 512)).astype(jnp.bfloat16)
        slots = call(
            own_modulation,
            shape((32, 8, 128), jnp.float32),
            active,
            jnp.transpose(mod_weight, (0, 2, 1)),
            scratch=[pltpu.VMEM((16, 128), jnp.float32)],
            smem=0,
        )
        groups = [
            [core * 128 + 16 * z_at + peer for core in range(2) for peer in range(16)]
            for z_at in range(ZS)
        ]
        slots = lax.all_to_all(slots, AXES, 0, 0, tiled=True, axis_index_groups=groups)
        far_rows, slots, tile, ids = after((far_rows, slots, tile, ids))

    with jax.named_scope("block"):
        other = call(
            split_weights, shape((3 * BLOCK, 384)), ids, near_rows, far_rows, query_weight
        )
        next_tile = send(tile, dyl=1)
        block = call(
            join_weights,
            shape((BLOCK_ROWS, 384)),
            ids,
            near_rows,
            far_rows,
            send(other, dc=1),
            query_weight,
            out_weight,
            slots,
        )
        block, next_tile, tile = after((block, next_tile, tile))

    with jax.named_scope("ring1"):
        right, left = send(block, dz=1), send(block, dz=-1)
        near = call(stack_rows, shape((2 * TILE, WIDTH)), tile, next_tile, smem=0)
        near_right, near_left = send(near, dx=1), send(near, dx=-1)
        text = lax.dynamic_slice_in_dim(
            hidden_text[0], jnp.minimum(TEXT_PART * z, 226 - TEXT_PART), TEXT_PART, 0
        )
        right, left, near_right, near_left, text = after(
            (right, left, near_right, near_left, text)
        )
    pieces = [block, right, left]

    with jax.named_scope("ring2"):
        right, left = send(right, dz=1), send(left, dz=-1)
        far_right, far_left = send(near_right[:TILE], dx=1), send(near_left[TILE:], dx=-1)
        text_other = send(text, dc=1)
        other_near = send(near, dc=1)
        right, left, far_right, far_left, text_other, other_near = after(
            (right, left, far_right, far_left, text_other, other_near)
        )
    pieces += [right, left]

    with jax.named_scope("ring3"):
        right, left = send(right, dz=1), send(left, dz=-1)
        other_right, other_left = send(near_right, dc=1), send(near_left, dc=1)
        far_right_other, far_left_other = send(far_right, dc=1), send(far_left, dc=1)
        first = call(
            norm_tokens, shape((4 * TILE, WIDTH), jnp.float32), near, other_near, smem=0
        )
        text = jnp.where(c == yh, text, text_other)
        average, partner = constant_matrices()
        cosine, sine = call(
            rotary_tables, [shape((KEYS, 256), jnp.float32)] * 2, ids, rotary_rates()
        )
        gains = jnp.tile(jnp.stack([query_gain, key_gain]), (1, 4))
        tables = (average, partner, cosine, sine, gains)
        others = (other_right, other_left, far_right_other, far_left_other)
        right, left, others, text, first, tables = after(
            (right, left, others, text, first, tables)
        )
        other_right, other_left, far_right_other, far_left_other = others
    pieces += [right, left]

    with jax.named_scope("ring4"):
        right = send(right[:CUT], dz=1)
        left = send(left[CUT:], dz=-1)
        second = call(
            norm_tokens,
            shape((8 * TILE, WIDTH), jnp.float32),
            near_right,
            near_left,
            other_right,
            other_left,
            smem=0,
        )
        third = call(
            norm_tokens,
            shape((5 * TILE, WIDTH), jnp.float32),
            far_right,
            far_left,
            far_right_other,
            far_left_other,
            text,
            smem=0,
        )
        right, left, second, third = after((right, left, second, third))

    with jax.named_scope("projections"):
        keys, inputs, query_low, query_high, out_near, modulation = call(
            project_keys,
            [
                shape((KEYS, 384)),
                shape((KEYS, WIDTH)),
                shape((ZS * HALF, 384)),
                shape((ZS * HALF, 384)),
                shape((ZS * BLOCK, 384)),
                shape((8, WIDTH), jnp.float32),
            ],
            ids,
            first,
            second,
            third,
            *pieces,
            right,
            left,
            *tables,
            scratch=[pltpu.VMEM((WIDTH, 384), jnp.bfloat16), pltpu.VMEM((ZS, 8, 384), jnp.float32)],
            flops=2 * KEYS * WIDTH * 384,
            room=32,
        )

    with jax.named_scope("attention"):
        state_shapes = [shape((3, VIDEO, 128), jnp.float32)] * 3
        cost = 4 * VIDEO * KEYS * 256 * 3
        rights, lefts = [], []

        def more(away, state):
            def body(*refs):
                attend_more(away, *refs)

            args = (ids, valid_count, query, rights[away - 1], lefts[away - 1], *state)
            return call(body, state_shapes, *args, smem=2, flops=2 * cost)

        right, left = send(keys, dz=1), send(keys, dz=-1)
        far_low, far_high = send(query_low, dyh=1), send(query_high, dyh=1)
        right, left, out_near = after((right, left, out_near))
        rights.append(right)
        lefts.append(left)

        right, left = send(right, dz=1), send(left, dz=-1)
        out_far = send(out_near, dyh=1)
        query = call(
            project_query,
            shape((VIDEO, 256)),
            ids,
            inputs,
            query_low,
            query_high,
            far_low,
            far_high,
            *tables,
            scratch=[pltpu.VMEM((WIDTH, 256), jnp.bfloat16)],
            flops=2 * VIDEO * WIDTH * 256,
            room=24,
        )
        state = call(
            attend_first, state_shapes, ids, valid_count, query, keys, smem=2, flops=cost
        )
        right, left, *state = after((right, left, *state))
        rights.append(right)
        lefts.append(left)

        right, left = send(right, dz=1), send(left, dz=-1)
        state = more(2, more(1, state))
        right, left, *state = after((right, left, *state))
        rights.append(right)
        lefts.append(left)

        right, left = send(right[: KEYS // 2], dz=1), send(left[KEYS // 2 :], dz=-1)
        state = more(3, state)
        last_weight = call(sort_out, shape((WIDTH // 2, 384)), ids, out_near, out_far)
        right, left, last_weight, *state = after((right, left, last_weight, *state))
        attended = call(
            attend_last,
            shape((VIDEO, 192)),
            ids,
            valid_count,
            query,
            right,
            left,
            *state,
            smem=2,
            flops=cost,
        )

    with jax.named_scope("output"):
        parts = call(
            project_out,
            shape((16, TILE, WIDTH // 2)),
            ids,
            attended,
            send(attended, dc=1),
            last_weight,
            modulation,
        )
        groups = [[16 * z_at + peer for peer in range(16)] for z_at in range(ZS)]
        parts = lax.all_to_all(
            parts, ("row", "col"), 0, 0, tiled=True, axis_index_groups=groups
        )
        own_sum, other_sum = call(
            sum_cols,
            [shape((TILE, WIDTH // 2), jnp.float32), shape((TILE, WIDTH // 2))],
            ids,
            parts,
        )
        result = call(
            finish_rows,
            shape((TILE, WIDTH)),
            ids,
            home_tile,
            own_sum,
            send(other_sum, dc=1),
        )
        return result.reshape(hidden_video.shape)


def solution(mesh):
    placed = (
        P("item", None, "row", "col", None),
        P("item", None, None),
        P(),
        P(),
        P(None, None, ("item", "row", "col")),
        P(("item", "row"), "col"),
        P(("item", "row"), "col"),
        P(("item", "row"), "col"),
        P(("item", "row"), "col"),
        P(),
        P(),
    )
    return jax.shard_map(
        on_device,
        mesh=mesh,
        in_specs=placed,
        out_specs=P("item", None, "row", "col", None),
        check_vma=False,
    )
```

```python
import math

import jax
import jax.numpy as jnp
import numpy as np
from jax import lax
from jax.experimental import pallas as pl
from jax.experimental.pallas import tpu as pltpu
from jax.sharding import PartitionSpec as P

AXES = ("item", "row", "col")
NEG_FILL = -1e30
WIDTH = 3072
BLOCK = 96
HALF = 48
TILE = 32
STRIP = 256
VIDEO = 512
TEXT_PART = 32
KEYS = VIDEO + TEXT_PART
ZS = 8


def place_of(device):
    c, row, col = device // 128, device // 8 % 16, device % 8
    return c, row // 2, row % 2, col // 2, col % 2


def device_of(c, z, yh, x, yl):
    return c % 2 * 128 + (z % 8 * 2 + yh % 2) * 8 + x % 4 * 2 + yl % 2


def send(values, dc=0, dz=0, dyh=0, dx=0, dyl=0):
    pairs = []
    for device in range(256):
        c, z, yh, x, yl = place_of(device)
        pairs.append((device, device_of(c + dc, z + dz, yh + dyh, x + dx, yl + dyl)))
    return lax.ppermute(values, AXES, pairs)


def trade_items(values):
    pairs = []
    for device in range(256):
        c, z, yh, x, yl = place_of(device)
        pairs.append((device, device_of(yh, z, c, x, yl)))
    return lax.ppermute(values, AXES, pairs)


def call(body, outs, *args, scratch=(), smem=1, flops=0, moved=0, room=12):
    specs = [pl.BlockSpec(memory_space=pltpu.SMEM)] * smem
    specs += [pl.BlockSpec(memory_space=pltpu.VMEM)] * (len(args) - smem)
    many = isinstance(outs, (list, tuple))
    out_specs = pl.BlockSpec(memory_space=pltpu.VMEM)
    return pl.pallas_call(
        body,
        out_shape=outs,
        in_specs=specs,
        out_specs=[out_specs] * len(outs) if many else out_specs,
        scratch_shapes=list(scratch),
        compiler_params=pltpu.CompilerParams(vmem_limit_bytes=room << 20),
        cost_estimate=pl.CostEstimate(flops=flops, bytes_accessed=moved, transcendentals=0),
    )(*args)


def shape(dims, dtype=jnp.bfloat16):
    return jax.ShapeDtypeStruct(dims, dtype)


def matmul(left, right):
    return jnp.dot(left, right, preferred_element_type=jnp.float32)


def matmul_nt(left, right):
    return lax.dot_general(
        left, right, (((1,), (1,)), ((), ())), preferred_element_type=jnp.float32
    )


MODS, KEYS_AT, QUERY_AT, OUT_AT, BLOCK_ROWS, CUT = 16, 16, 400, 496, 592, 304


def heads_of(values, first):
    values = values.astype(jnp.float32)
    return jnp.where(first, values[:, :192], values[:, 192:])


def stack_rows(first_ref, second_ref, out_ref):
    count = first_ref.shape[0]
    out_ref[:count, :] = first_ref[...]
    out_ref[count:, :] = second_ref[...]


def split_weights(ids, near_ref, far_ref, query_ref, other_ref):
    second = ids[0] != 0
    for ref, yh in ((near_ref, ids[2]), (far_ref, 1 - ids[2])):
        rows = pl.ds(pl.multiple_of(yh * BLOCK, 32), BLOCK)
        parts = [heads_of(ref[at * BLOCK : at * BLOCK + BLOCK, :], second) for at in range(2)]
        other_ref[rows, :] = jnp.concatenate(parts, axis=1).astype(jnp.bfloat16)
    query = heads_of(query_ref[...], second)
    other_ref[2 * BLOCK :, :] = jnp.concatenate([query, query], axis=1).astype(jnp.bfloat16)


def join_weights(
    ids, near_ref, far_ref, other_ref, query_ref, out_ref, slots_ref, block_ref
):
    c, yh = ids[0], ids[2]
    first = c == 0
    for ref, at in ((near_ref, yh), (far_ref, 1 - yh)):
        at = pl.multiple_of(at * BLOCK, 32)
        parts = [heads_of(ref[at * BLOCK : at * BLOCK + BLOCK, :], first) for at in range(2)]
        start = pl.multiple_of(KEYS_AT + c * 192 + at, 16)
        block_ref[pl.ds(start, BLOCK), :] = jnp.concatenate(parts, axis=1).astype(jnp.bfloat16)
        start = pl.multiple_of(KEYS_AT + (1 - c) * 192 + at, 16)
        block_ref[pl.ds(start, BLOCK), :] = other_ref[pl.ds(at, BLOCK), :]
    query = heads_of(query_ref[...], first)
    other = other_ref[2 * BLOCK :, :].astype(jnp.float32)[:, :192]
    low, high = jnp.where(first, query, other), jnp.where(first, other, query)
    block_ref[QUERY_AT:OUT_AT, :] = jnp.concatenate([low, high], axis=1).astype(jnp.bfloat16)
    block_ref[OUT_AT:, :] = out_ref[...]
    full = jnp.concatenate([slots_ref[peer][:, :12] for peer in range(32)], axis=1)
    high = full.astype(jnp.bfloat16).astype(jnp.float32)
    middle = (full - high).astype(jnp.bfloat16).astype(jnp.float32)
    low = full - high - middle
    rows = [term[part : part + 1, :] for term in (high, middle, low) for part in range(5)]
    rows.append(jnp.zeros_like(rows[0]))
    block_ref[:MODS, :] = jnp.concatenate(rows, axis=0).astype(jnp.bfloat16)


AWAY = (0, -1, 1, -2, 2, -3, 3)


def sort_out(ids, near_ref, far_ref, weight_ref):
    for ref, yh in ((near_ref, ids[2]), (far_ref, 1 - ids[2])):
        for z in range(ZS):
            rows = pl.ds(pl.multiple_of(z * 192 + yh * BLOCK, 32), BLOCK)
            weight_ref[rows, :] = ref[z * BLOCK : z * BLOCK + BLOCK, :]


def time_features(steps_in, embed_width):
    half_width = embed_width // 2
    rates = jnp.exp(-math.log(10000.0) * jnp.arange(half_width, dtype=jnp.float32) / half_width)
    phases = steps_in.astype(jnp.float32)[:, None] * rates[None, :]
    return jnp.concatenate([jnp.cos(phases), jnp.sin(phases)], axis=1)


def own_modulation(active_ref, weight_ref, slots_ref, tile_ref):
    tile_ref[...] = jnp.zeros_like(tile_ref)
    for part in range(6):
        both = matmul_nt(active_ref[...], weight_ref[part])
        for item in range(2):
            at = item * 8 + part
            tile_ref[at : at + 1, :12] = both[item : item + 1, :]
    for peer in range(32):
        item = peer // 8 % 2
        slots_ref[peer] = tile_ref[item * 8 : item * 8 + 8, :]


def layer_norm(values, epsilon):
    center = values - jnp.mean(values, axis=-1, keepdims=True)
    spread = jnp.mean(center * center, axis=-1, keepdims=True)
    return center * lax.rsqrt(spread + epsilon)


def split_dot(values, constant):
    high = values.astype(jnp.bfloat16)
    low = (values - high.astype(jnp.float32)).astype(jnp.bfloat16)
    return matmul(high, constant) + matmul(low, constant)


def norm_and_rotate(raw, gain, average, partner, cosine, sine):
    center = raw - split_dot(raw, average)
    spread = split_dot(center * center, average)
    normed = center * lax.rsqrt(spread + 1e-06) * jnp.concatenate([gain] * 4, axis=1)
    return normed * cosine + split_dot(normed, partner) * sine


def norm_tokens(*refs):
    start = 0
    for ref in refs[:-1]:

        def step(at, _, ref=ref, start=start):
            at = pl.multiple_of(at * 16, 16)
            refs[-1][pl.ds(pl.multiple_of(start + at, 16), 16), :] = layer_norm(
                ref[pl.ds(at, 16), :].astype(jnp.float32), 1e-05
            )
            return 0

        lax.fori_loop(0, ref.shape[0] // 16, step, 0, unroll=2)
        start += ref.shape[0]


TILES = (
    ((0, 0, 0), (0, 1, 0), (0, 0, 1), (0, 1, 1)),
    (
        (-1, 0, 0),
        (-1, 1, 0),
        (1, 0, 0),
        (1, 1, 0),
        (-1, 0, 1),
        (-1, 1, 1),
        (1, 0, 1),
        (1, 1, 1),
    ),
    ((-2, 0, 0), (2, 1, 0), (-2, 0, 1), (2, 1, 1)),
)


def project_keys(ids, first_ref, second_ref, third_ref, *refs):
    c, z, x, yl = ids[0], ids[1], ids[3], ids[4]
    pieces, rest = refs[:9], refs[9:]
    (average_ref, partner_ref, cosine_ref, sine_ref, gain_ref) = rest[:5]
    keys_out, input_out, low_out, high_out, out_out, mod_ref, weight_ref, terms_ref = rest[5:]
    places = [(z + dz + ZS) % ZS for dz in AWAY + (4,)]
    for ref, place in zip(pieces[:8], places):
        terms = ref[:MODS, :].astype(jnp.float32)
        terms_ref[place] = jnp.concatenate(
            [terms[:5] + terms[5:10] + terms[10:15], jnp.zeros((3, 384), jnp.float32)], axis=0
        )
    for core in range(2):
        mods = [terms_ref[place][:, core * 192 : core * 192 + 192] for place in range(ZS)]
        mod_ref[:, core * 1536 : core * 1536 + 1536] = jnp.concatenate(mods, axis=1)
    for ref, place in zip(pieces[:7] + pieces[8:], places):
        at = ref.shape[0] - 2 * BLOCK
        rows = pl.ds(pl.multiple_of(place * BLOCK, 32), BLOCK)
        out_out[rows, :] = ref[at + BLOCK :, :]
        rows = pl.ds(pl.multiple_of(place * HALF, 16), HALF)
        low_out[rows, :] = ref[at : at + HALF, :]
        high_out[rows, :] = ref[at + HALF : at + BLOCK, :]
    moves = []
    for ref, tiles in zip((first_ref, second_ref, third_ref), TILES):
        for at, (dx, part, core) in enumerate(tiles):
            col = (x + dx + 4) % 4 * 2 + (yl + part) % 2
            moves.append((ref, at * TILE, (c + core) % 2 * STRIP + col * TILE, 0))
    moves.append((third_ref, 4 * TILE, VIDEO, 3))
    for ref, source, target, part in moves:
        scale, shift = 1.0 + mod_ref[part + 1 : part + 2, :], mod_ref[part : part + 1, :]
        for at in (0, 16):
            rows = ref[source + at : source + at + 16, :] * scale + shift
            input_out[pl.ds(pl.multiple_of(target + at, 16), 16), :] = rows.astype(jnp.bfloat16)
    for ref, place in zip(pieces[:7], places):
        for core in range(2):
            start = pl.multiple_of(core * 1536 + place * 192, 32)
            at = KEYS_AT + core * 192
            weight_ref[pl.ds(start, 192), :] = ref[at : at + 192, :]
    right_ref, left_ref, place = pieces[7], pieces[8], places[7]
    start = pl.multiple_of(place * 192, 32)
    weight_ref[pl.ds(start, 192), :] = right_ref[KEYS_AT : KEYS_AT + 192, :]
    start = pl.multiple_of(1536 + place * 192, 32)
    weight_ref[pl.ds(start, BLOCK), :] = right_ref[KEYS_AT + 192 :, :]
    start = pl.multiple_of(1536 + place * 192 + BLOCK, 32)
    weight_ref[pl.ds(start, BLOCK), :] = left_ref[:BLOCK, :]
    raw = matmul(input_out[...], weight_ref[...])
    lanes = lax.broadcasted_iota(jnp.int32, (1, 256), 1)
    key_raw = raw[:, :256]
    key = norm_and_rotate(
        key_raw,
        gain_ref[...],
        average_ref[...],
        partner_ref[...],
        cosine_ref[...],
        sine_ref[...],
    )
    keys_out[:, :256] = jnp.where(lanes < 192, key, key_raw).astype(jnp.bfloat16)
    keys_out[:, 256:] = raw[:, 256:384].astype(jnp.bfloat16)


def project_query(ids, input_ref, near_low, near_high, far_low, far_high, *refs):
    average_ref, partner_ref, cosine_ref, sine_ref, gain_ref, out, weight_ref = refs
    weight_ref[:, 192:] = jnp.zeros((WIDTH, 64), jnp.bfloat16)
    yh = ids[2]
    for ref, at in (
        (near_low, yh * BLOCK),
        (near_high, yh * BLOCK + HALF),
        (far_low, (1 - yh) * BLOCK),
        (far_high, (1 - yh) * BLOCK + HALF),
    ):
        for z in range(ZS):
            values = ref[z * HALF : z * HALF + HALF, :].astype(jnp.float32)
            for core in range(2):
                start = pl.multiple_of(core * 1536 + z * 192 + at, 16)
                weight_ref[pl.ds(start, HALF), :192] = values[
                    :, core * 192 : core * 192 + 192
                ].astype(jnp.bfloat16)
    raw = matmul(input_ref[:VIDEO, :], weight_ref[...])
    query = norm_and_rotate(
        raw,
        gain_ref[...],
        average_ref[...],
        partner_ref[...],
        cosine_ref[:VIDEO, :],
        sine_ref[:VIDEO, :],
    )
    out[...] = (query.astype(jnp.bfloat16).astype(jnp.float32) * 0.125).astype(jnp.bfloat16)


def rotary_tables(ids, rate_ref, cosine_ref, sine_ref):
    token = lax.broadcasted_iota(jnp.int32, (KEYS, 256), 0)
    lane = lax.broadcasted_iota(jnp.int32, (KEYS, 256), 1) % 64
    frame = token % 32 // 8
    height = 4 * ids[1] + token // 256 * 2 + token % 8 // 4
    across = token % 256 // 32 * 4 + token % 4
    place = jnp.where(lane < 16, frame, jnp.where(lane < 40, height, across))
    angle = jnp.where(token < VIDEO, place.astype(jnp.float32) * rate_ref[...], 0.0)
    back = jnp.logical_or(
        jnp.logical_and(lane >= 8, lane < 16),
        jnp.logical_or(jnp.logical_and(lane >= 28, lane < 40), lane >= 52),
    )
    cosine_ref[...] = jnp.cos(angle)
    sine = jnp.sin(angle)
    sine_ref[...] = jnp.where(back, sine, -sine)


def usable_bias(count, first, z, limit):
    token = lax.broadcasted_iota(jnp.int32, (count, 128), 0) + first
    height = 4 * z + token // 256 * 2 + token % 8 // 4
    index = (token % 32 // 8 * 32 + height) * 32 + token % 256 // 32 * 4 + token % 4
    video_ok = jnp.logical_and(token < VIDEO, index < limit)
    text_at = jnp.minimum(TEXT_PART * z, 226 - TEXT_PART) + token - VIDEO
    text_ok = jnp.logical_and(token >= VIDEO, text_at >= TEXT_PART * z)
    return jnp.where(jnp.logical_or(video_ok, text_ok), 0.0, NEG_FILL).astype(jnp.bfloat16)


def attend_pieces(ids, counts, query_ref, pieces, old, new, finish):
    z, limit = ids[1], counts[ids[2]]
    loaded = []
    for ref, dz, first, count in pieces:
        values = ref[...]
        bias = usable_bias(count, first, (z + dz + ZS) % ZS, limit)
        loaded.append((values, bias))
    values = jnp.concatenate([entry[0] for entry in loaded], axis=0)
    bias = jnp.concatenate([entry[1] for entry in loaded], axis=0)
    ones = jnp.ones(bias.shape, jnp.bfloat16)
    lanes = lax.broadcasted_iota(jnp.int32, (1, 128), 1)
    pick = jnp.where(lanes == 0, 1.0, 0.0).astype(jnp.bfloat16)
    keys = [jnp.concatenate([values[:, at : at + 128], bias], axis=1) for at in (0, 128)]
    mixes = [jnp.concatenate([values[:, at : at + 128], ones], axis=1) for at in (128, 256)]
    for start in range(0, VIDEO, STRIP):
        rows = slice(start, start + STRIP)
        finished = []
        for head in range(3):
            key_tile, mix_tile = (0, 0, 1)[head], (0, 1, 1)[head]
            inside = (lanes < 64) if head != 1 else (lanes >= 64)
            query = query_ref[rows, key_tile * 128 : key_tile * 128 + 128]
            query = jnp.where(inside, query, jnp.zeros_like(query))
            query = jnp.concatenate([query, jnp.broadcast_to(pick, query.shape)], axis=1)
            scores = matmul_nt(query, keys[key_tile])
            best = jnp.max(scores, axis=1, keepdims=True)
            if old is None:
                powers = jnp.exp(scores - best).astype(jnp.bfloat16)
                mixed = matmul(powers, mixes[mix_tile])
                gathered, total = mixed[:, :128], mixed[:, 128:]
                best = jnp.broadcast_to(best, gathered.shape)
            else:
                best_old = old[0][head, rows, :]
                best = jnp.maximum(best_old, best)
                powers = jnp.exp(scores - best[:, :1]).astype(jnp.bfloat16)
                mixed = matmul(powers, mixes[mix_tile])
                rescale = jnp.exp(best_old - best)
                total = old[1][head, rows, :] * rescale + mixed[:, 128:]
                gathered = old[2][head, rows, :] * rescale + mixed[:, :128]
            if finish is None:
                new[0][head, rows, :] = best
                new[1][head, rows, :] = total
                new[2][head, rows, :] = gathered
            else:
                finished.append(gathered / total)
        if finish is not None:
            finish[rows, :] = jnp.concatenate(
                [finished[0][:, 64:], finished[1][:, :64], finished[2][:, 64:]], axis=1
            ).astype(jnp.bfloat16)


def attend_first(ids, counts, query_ref, own_ref, *new):
    attend_pieces(ids, counts, query_ref, [(own_ref, 0, 0, KEYS)], None, new, None)


def attend_more(dz, ids, counts, query_ref, right_ref, left_ref, *states):
    pieces = [(right_ref, -dz, 0, KEYS), (left_ref, dz, 0, KEYS)]
    attend_pieces(ids, counts, query_ref, pieces, states[:3], states[3:], None)


def attend_last(ids, counts, query_ref, right_ref, left_ref, best, total, gathered, out_ref):
    half = KEYS // 2
    pieces = [(right_ref, -4, 0, half), (left_ref, 4, half, half)]
    attend_pieces(ids, counts, query_ref, pieces, (best, total, gathered), None, out_ref)


def project_out(ids, own_ref, other_ref, weight_ref, mod_ref, out_ref):
    first = ids[0] == 0
    half = WIDTH // 2
    gate = mod_ref[2:3, pl.ds(pl.multiple_of(ids[0] * half, half), half)]
    weight = weight_ref[...]
    for row in range(2):
        rows = slice(row * STRIP, row * STRIP + STRIP)
        own, other = own_ref[rows, :].astype(jnp.float32), other_ref[rows, :].astype(jnp.float32)
        attended = jnp.concatenate(
            [jnp.where(first, own, other), jnp.where(first, other, own)], axis=1
        ).astype(jnp.bfloat16)
        gated = (matmul_nt(attended, weight) * gate).astype(jnp.bfloat16)
        for col in range(8):
            out_ref[row * 8 + col] = gated[col * TILE : col * TILE + TILE, :]


def sum_cols(ids, parts_ref, own_ref, other_ref):
    for ref, item in ((own_ref, ids[0]), (other_ref, 1 - ids[0])):
        total = parts_ref[item * 8].astype(jnp.float32)
        for peer in range(1, 8):
            total += parts_ref[item * 8 + peer].astype(jnp.float32)
        ref[...] = total.astype(ref.dtype)


def finish_rows(ids, hidden_ref, own_ref, other_ref, out_ref):
    first = ids[0] == 0
    half = WIDTH // 2
    own, other = own_ref[...], other_ref[...].astype(jnp.float32)
    low, high = jnp.where(first, own, other), jnp.where(first, other, own)
    out_ref[:, :half] = (hidden_ref[:, :half].astype(jnp.float32) + low).astype(jnp.bfloat16)
    out_ref[:, half:] = (hidden_ref[:, half:].astype(jnp.float32) + high).astype(jnp.bfloat16)


def rotary_rates():
    rates = []
    for band in (16, 24, 24):
        half = band // 2
        rate = np.exp(-math.log(10000.0) * (2.0 * np.arange(half) / band)).astype(np.float32)
        rates += [rate, rate]
    return jnp.asarray(np.tile(np.concatenate(rates), 4)[None, :])


def constant_matrices():
    average = np.zeros((256, 256), np.float32)
    partner = np.zeros((256, 256), np.float32)
    for head in range(4):
        average[head * 64 : head * 64 + 64, head * 64 : head * 64 + 64] = 1.0 / 64
        at = head * 64
        for band in (16, 24, 24):
            half = band // 2
            for entry in range(half):
                partner[at + half + entry, at + entry] = 1.0
                partner[at + entry, at + half + entry] = 1.0
            at += band
    return jnp.asarray(average, jnp.bfloat16), jnp.asarray(partner, jnp.bfloat16)


def on_device(
    hidden_video,
    hidden_text,
    step,
    valid_count,
    mod_weight,
    query_weight,
    key_weight,
    value_weight,
    out_weight,
    query_gain,
    key_gain,
):
    c = lax.axis_index("item")
    row = lax.axis_index("row")
    col = lax.axis_index("col")
    z, yh = row // 2, row % 2
    ids = jnp.stack([c, z, yh, col // 2, col % 2]).astype(jnp.int32)
    after = lax.optimization_barrier

    with jax.named_scope("start"):
        near_rows = call(stack_rows, shape((2 * BLOCK, 384)), key_weight, value_weight, smem=0)
        far_rows = send(near_rows, dyh=1)
        home_tile = hidden_video.reshape(TILE, WIDTH)
        tile = trade_items(home_tile)
        active = jax.nn.silu(time_features(step, 512)).astype(jnp.bfloat16)
        slots = call(
            own_modulation,
            shape((32, 8, 128), jnp.float32),
            active,
            jnp.transpose(mod_weight, (0, 2, 1)),
            scratch=[pltpu.VMEM((16, 128), jnp.float32)],
            smem=0,
        )
        groups = [
            [core * 128 + 16 * z_at + peer for core in range(2) for peer in range(16)]
            for z_at in range(ZS)
        ]
        slots = lax.all_to_all(slots, AXES, 0, 0, tiled=True, axis_index_groups=groups)
        far_rows, slots, tile, ids = after((far_rows, slots, tile, ids))

    with jax.named_scope("block"):
        other = call(
            split_weights, shape((3 * BLOCK, 384)), ids, near_rows, far_rows, query_weight
        )
        next_tile = send(tile, dyl=1)
        block = call(
            join_weights,
            shape((BLOCK_ROWS, 384)),
            ids,
            near_rows,
            far_rows,
            send(other, dc=1),
            query_weight,
            out_weight,
            slots,
        )
        block, tile = after((block, tile))

    with jax.named_scope("ring1"):
        right, left = send(block, dz=1), send(block, dz=-1)
        near = call(stack_rows, shape((2 * TILE, WIDTH)), tile, next_tile, smem=0)
        near_right, near_left = send(near, dx=1), send(near, dx=-1)
        text = lax.dynamic_slice_in_dim(
            hidden_text[0], jnp.minimum(TEXT_PART * z, 226 - TEXT_PART), TEXT_PART, 0
        )
        right, left, near_right, near_left, text = after(
            (right, left, near_right, near_left, text)
        )
    pieces = [block, right, left]

    with jax.named_scope("ring2"):
        right, left = send(right, dz=1), send(left, dz=-1)
        far_right, far_left = send(near_right[:TILE], dx=1), send(near_left[TILE:], dx=-1)
        text_other = send(text, dc=1)
        other_near = send(near, dc=1)
        right, left, far_right, far_left, text_other, other_near = after(
            (right, left, far_right, far_left, text_other, other_near)
        )
    pieces += [right, left]

    with jax.named_scope("ring3"):
        right, left = send(right, dz=1), send(left, dz=-1)
        other_right, other_left = send(near_right, dc=1), send(near_left, dc=1)
        far_right_other, far_left_other = send(far_right, dc=1), send(far_left, dc=1)
        first = call(
            norm_tokens, shape((4 * TILE, WIDTH), jnp.float32), near, other_near, smem=0
        )
        text = jnp.where(c == yh, text, text_other)
        average, partner = constant_matrices()
        cosine, sine = call(
            rotary_tables, [shape((KEYS, 256), jnp.float32)] * 2, ids, rotary_rates()
        )
        tables = (average, partner, cosine, sine)
        others = (other_right, other_left, far_right_other, far_left_other)
        right, left, others, text, first, tables = after(
            (right, left, others, text, first, tables)
        )
        other_right, other_left, far_right_other, far_left_other = others
    pieces += [right, left]

    with jax.named_scope("ring4"):
        right = send(right[:CUT], dz=1)
        left = send(left[CUT:], dz=-1)
        second = call(
            norm_tokens,
            shape((8 * TILE, WIDTH), jnp.float32),
            near_right,
            near_left,
            other_right,
            other_left,
            smem=0,
        )
        third = call(
            norm_tokens,
            shape((5 * TILE, WIDTH), jnp.float32),
            far_right,
            far_left,
            far_right_other,
            far_left_other,
            text,
            smem=0,
        )
        right, left, second, third = after((right, left, second, third))

    with jax.named_scope("projections"):
        keys, inputs, query_low, query_high, out_near, modulation = call(
            project_keys,
            [
                shape((KEYS, 384)),
                shape((KEYS, WIDTH)),
                shape((ZS * HALF, 384)),
                shape((ZS * HALF, 384)),
                shape((ZS * BLOCK, 384)),
                shape((8, WIDTH), jnp.float32),
            ],
            ids,
            first,
            second,
            third,
            *pieces,
            right,
            left,
            *tables,
            key_gain[None, :],
            scratch=[pltpu.VMEM((WIDTH, 384), jnp.bfloat16), pltpu.VMEM((ZS, 8, 384), jnp.float32)],
            flops=2 * KEYS * WIDTH * 384,
            room=32,
        )

    with jax.named_scope("attention"):
        state_shapes = [shape((3, VIDEO, 128), jnp.float32)] * 3
        cost = 4 * VIDEO * KEYS * 256 * 3
        rights, lefts = [], []

        def more(away, state):
            def body(*refs):
                attend_more(away, *refs)

            args = (ids, valid_count, query, rights[away - 1], lefts[away - 1], *state)
            return call(body, state_shapes, *args, smem=2, flops=2 * cost)

        right, left = send(keys, dz=1), send(keys, dz=-1)
        far_low, far_high = send(query_low, dyh=1), send(query_high, dyh=1)
        right, left, out_near = after((right, left, out_near))
        rights.append(right)
        lefts.append(left)

        right, left = send(right, dz=1), send(left, dz=-1)
        out_far = send(out_near, dyh=1)
        query = call(
            project_query,
            shape((VIDEO, 256)),
            ids,
            inputs,
            query_low,
            query_high,
            far_low,
            far_high,
            *tables,
            query_gain[None, :],
            scratch=[pltpu.VMEM((WIDTH, 256), jnp.bfloat16)],
            flops=2 * VIDEO * WIDTH * 256,
            room=24,
        )
        state = call(
            attend_first, state_shapes, ids, valid_count, query, keys, smem=2, flops=cost
        )
        right, left, *state = after((right, left, *state))
        rights.append(right)
        lefts.append(left)

        right, left = send(right, dz=1), send(left, dz=-1)
        state = more(2, more(1, state))
        right, left, *state = after((right, left, *state))
        rights.append(right)
        lefts.append(left)

        right, left = send(right[: KEYS // 2], dz=1), send(left[KEYS // 2 :], dz=-1)
        state = more(3, state)
        last_weight = call(sort_out, shape((WIDTH // 2, 384)), ids, out_near, out_far)
        right, left, last_weight, *state = after((right, left, last_weight, *state))
        attended = call(
            attend_last,
            shape((VIDEO, 192)),
            ids,
            valid_count,
            query,
            right,
            left,
            *state,
            smem=2,
            flops=cost,
        )

    with jax.named_scope("output"):
        parts = call(
            project_out,
            shape((16, TILE, WIDTH // 2)),
            ids,
            attended,
            send(attended, dc=1),
            last_weight,
            modulation,
        )
        groups = [[16 * z_at + peer for peer in range(16)] for z_at in range(ZS)]
        parts = lax.all_to_all(
            parts, ("row", "col"), 0, 0, tiled=True, axis_index_groups=groups
        )
        own_sum, other_sum = call(
            sum_cols,
            [shape((TILE, WIDTH // 2), jnp.float32), shape((TILE, WIDTH // 2))],
            ids,
            parts,
        )
        result = call(
            finish_rows,
            shape((TILE, WIDTH)),
            ids,
            home_tile,
            own_sum,
            send(other_sum, dc=1),
        )
        return result.reshape(hidden_video.shape)


def solution(mesh):
    placed = (
        P("item", None, "row", "col", None),
        P("item", None, None),
        P(),
        P(),
        P(None, None, ("item", "row", "col")),
        P(("item", "row"), "col"),
        P(("item", "row"), "col"),
        P(("item", "row"), "col"),
        P(("item", "row"), "col"),
        P(),
        P(),
    )
    return jax.shard_map(
        on_device,
        mesh=mesh,
        in_specs=placed,
        out_specs=P("item", None, "row", "col", None),
        check_vma=False,
    )
```

```python
import math

import jax
import jax.numpy as jnp
import numpy as np
from jax import lax
from jax.experimental import pallas as pl
from jax.experimental.pallas import tpu as pltpu
from jax.sharding import PartitionSpec as P

AXES = ("item", "row", "col")
NEG_FILL = -1e30
WIDTH = 3072
BLOCK = 96
HALF = 48
TILE = 32
STRIP = 256
VIDEO = 512
TEXT_PART = 32
QUERIES = 256
KEYS = VIDEO + TEXT_PART
ZS = 8


def place_of(device):
    c, row, col = device // 128, device // 8 % 16, device % 8
    return c, row // 2, row % 2, col // 2, col % 2


def device_of(c, z, yh, x, yl):
    return c % 2 * 128 + (z % 8 * 2 + yh % 2) * 8 + x % 4 * 2 + yl % 2


def send(values, dc=0, dz=0, dyh=0, dx=0, dyl=0):
    pairs = []
    for device in range(256):
        c, z, yh, x, yl = place_of(device)
        pairs.append((device, device_of(c + dc, z + dz, yh + dyh, x + dx, yl + dyl)))
    return lax.ppermute(values, AXES, pairs)


def trade_items(values):
    pairs = []
    for device in range(256):
        c, z, yh, x, yl = place_of(device)
        pairs.append((device, device_of(yh, z, c, x, yl)))
    return lax.ppermute(values, AXES, pairs)


def call(body, outs, *args, scratch=(), smem=1, flops=0, moved=0, room=12):
    specs = [pl.BlockSpec(memory_space=pltpu.SMEM)] * smem
    specs += [pl.BlockSpec(memory_space=pltpu.VMEM)] * (len(args) - smem)
    many = isinstance(outs, (list, tuple))
    out_specs = pl.BlockSpec(memory_space=pltpu.VMEM)
    return pl.pallas_call(
        body,
        out_shape=outs,
        in_specs=specs,
        out_specs=[out_specs] * len(outs) if many else out_specs,
        scratch_shapes=list(scratch),
        compiler_params=pltpu.CompilerParams(vmem_limit_bytes=room << 20),
        cost_estimate=pl.CostEstimate(flops=flops, bytes_accessed=moved, transcendentals=0),
    )(*args)


def shape(dims, dtype=jnp.bfloat16):
    return jax.ShapeDtypeStruct(dims, dtype)


def matmul(left, right):
    return jnp.dot(left, right, preferred_element_type=jnp.float32)


def matmul_nt(left, right):
    return lax.dot_general(
        left, right, (((1,), (1,)), ((), ())), preferred_element_type=jnp.float32
    )


MODS, KEYS_AT, QUERY_AT, OUT_AT, BLOCK_ROWS, CUT = 16, 16, 400, 496, 592, 304


def heads_of(values, first):
    values = values.astype(jnp.float32)
    return jnp.where(first, values[:, :192], values[:, 192:])


def stack_rows(first_ref, second_ref, out_ref):
    count = first_ref.shape[0]
    out_ref[:count, :] = first_ref[...]
    out_ref[count:, :] = second_ref[...]


def split_weights(ids, near_ref, far_ref, query_ref, other_ref):
    second = ids[0] != 0
    for ref, yh in ((near_ref, ids[2]), (far_ref, 1 - ids[2])):
        rows = pl.ds(pl.multiple_of(yh * BLOCK, 32), BLOCK)
        parts = [heads_of(ref[at * BLOCK : at * BLOCK + BLOCK, :], second) for at in range(2)]
        other_ref[rows, :] = jnp.concatenate(parts, axis=1).astype(jnp.bfloat16)
    query = heads_of(query_ref[...], second)
    other_ref[2 * BLOCK :, :] = jnp.concatenate([query, query], axis=1).astype(jnp.bfloat16)


def join_weights(
    ids, near_ref, far_ref, other_ref, query_ref, out_ref, slots_ref, block_ref
):
    c, yh = ids[0], ids[2]
    first = c == 0
    for ref, at in ((near_ref, yh), (far_ref, 1 - yh)):
        at = pl.multiple_of(at * BLOCK, 32)
        parts = [heads_of(ref[at * BLOCK : at * BLOCK + BLOCK, :], first) for at in range(2)]
        start = pl.multiple_of(KEYS_AT + c * 192 + at, 16)
        block_ref[pl.ds(start, BLOCK), :] = jnp.concatenate(parts, axis=1).astype(jnp.bfloat16)
        start = pl.multiple_of(KEYS_AT + (1 - c) * 192 + at, 16)
        block_ref[pl.ds(start, BLOCK), :] = other_ref[pl.ds(at, BLOCK), :]
    query = heads_of(query_ref[...], first)
    other = other_ref[2 * BLOCK :, :].astype(jnp.float32)[:, :192]
    low, high = jnp.where(first, query, other), jnp.where(first, other, query)
    block_ref[QUERY_AT:OUT_AT, :] = jnp.concatenate([low, high], axis=1).astype(jnp.bfloat16)
    block_ref[OUT_AT:, :] = out_ref[...]
    full = jnp.concatenate([slots_ref[peer][:, :12] for peer in range(32)], axis=1)
    high = full.astype(jnp.bfloat16).astype(jnp.float32)
    middle = (full - high).astype(jnp.bfloat16).astype(jnp.float32)
    low = full - high - middle
    rows = [term[part : part + 1, :] for term in (high, middle, low) for part in range(5)]
    rows.append(jnp.zeros_like(rows[0]))
    block_ref[:MODS, :] = jnp.concatenate(rows, axis=0).astype(jnp.bfloat16)


AWAY = (0, -1, 1, -2, 2, -3, 3)


def sort_out(ids, near_ref, far_ref, weight_ref):
    for ref, yh in ((near_ref, ids[2]), (far_ref, 1 - ids[2])):
        for z in range(ZS):
            rows = pl.ds(pl.multiple_of(z * 192 + yh * BLOCK, 32), BLOCK)
            weight_ref[rows, :] = ref[z * BLOCK : z * BLOCK + BLOCK, :]


def time_features(steps_in, embed_width):
    half_width = embed_width // 2
    rates = jnp.exp(-math.log(10000.0) * jnp.arange(half_width, dtype=jnp.float32) / half_width)
    phases = steps_in.astype(jnp.float32)[:, None] * rates[None, :]
    return jnp.concatenate([jnp.cos(phases), jnp.sin(phases)], axis=1)


def own_modulation(active_ref, weight_ref, slots_ref, tile_ref):
    tile_ref[...] = jnp.zeros_like(tile_ref)
    for part in range(6):
        both = matmul_nt(active_ref[...], weight_ref[part])
        for item in range(2):
            at = item * 8 + part
            tile_ref[at : at + 1, :12] = both[item : item + 1, :]
    for peer in range(32):
        item = peer // 8 % 2
        slots_ref[peer] = tile_ref[item * 8 : item * 8 + 8, :]


def layer_norm(values, epsilon):
    center = values - jnp.mean(values, axis=-1, keepdims=True)
    spread = jnp.mean(center * center, axis=-1, keepdims=True)
    return center * lax.rsqrt(spread + epsilon)


def split_dot(values, constant):
    high = values.astype(jnp.bfloat16)
    low = (values - high.astype(jnp.float32)).astype(jnp.bfloat16)
    return matmul(high, constant) + matmul(low, constant)


def norm_and_rotate(raw, gain, average, partner, cosine, sine):
    center = raw - split_dot(raw, average)
    spread = split_dot(center * center, average)
    normed = center * lax.rsqrt(spread + 1e-06) * jnp.concatenate([gain] * 4, axis=1)
    return normed * cosine + split_dot(normed, partner) * sine


def norm_tokens(*refs):
    start = 0
    for ref in refs[:-1]:

        def step(at, _, ref=ref, start=start):
            at = pl.multiple_of(at * 16, 16)
            refs[-1][pl.ds(pl.multiple_of(start + at, 16), 16), :] = layer_norm(
                ref[pl.ds(at, 16), :].astype(jnp.float32), 1e-05
            )
            return 0

        lax.fori_loop(0, ref.shape[0] // 16, step, 0, unroll=2)
        start += ref.shape[0]


TILES = (
    ((0, 0, 0), (0, 1, 0), (0, 0, 1), (0, 1, 1)),
    (
        (-1, 0, 0),
        (-1, 1, 0),
        (1, 0, 0),
        (1, 1, 0),
        (-1, 0, 1),
        (-1, 1, 1),
        (1, 0, 1),
        (1, 1, 1),
    ),
    ((-2, 0, 0), (2, 1, 0), (-2, 0, 1), (2, 1, 1)),
)


def project_keys(ids, first_ref, second_ref, third_ref, *refs):
    c, z, x, yl = ids[0], ids[1], ids[3], ids[4]
    pieces, rest = refs[:9], refs[9:]
    (average_ref, partner_ref, cosine_ref, sine_ref, gain_ref) = rest[:5]
    keys_out, input_out, low_out, high_out, out_out, mod_ref, weight_ref, terms_ref = rest[5:]
    places = [(z + dz + ZS) % ZS for dz in AWAY + (4,)]
    for ref, place in zip(pieces[:8], places):
        terms = ref[:MODS, :].astype(jnp.float32)
        terms_ref[place] = jnp.concatenate(
            [terms[:5] + terms[5:10] + terms[10:15], jnp.zeros((3, 384), jnp.float32)], axis=0
        )
    for core in range(2):
        mods = [terms_ref[place][:, core * 192 : core * 192 + 192] for place in range(ZS)]
        mod_ref[:, core * 1536 : core * 1536 + 1536] = jnp.concatenate(mods, axis=1)
    for ref, place in zip(pieces[:7] + pieces[8:], places):
        at = ref.shape[0] - 2 * BLOCK
        rows = pl.ds(pl.multiple_of(place * BLOCK, 32), BLOCK)
        out_out[rows, :] = ref[at + BLOCK :, :]
        rows = pl.ds(pl.multiple_of(place * HALF, 16), HALF)
        low_out[rows, :] = ref[at : at + HALF, :]
        high_out[rows, :] = ref[at + HALF : at + BLOCK, :]
    moves = []
    for ref, tiles in zip((first_ref, second_ref, third_ref), TILES):
        for at, (dx, part, core) in enumerate(tiles):
            col = (x + dx + 4) % 4 * 2 + (yl + part) % 2
            moves.append((ref, at * TILE, (c + core) % 2 * STRIP + col * TILE, 0))
    moves.append((third_ref, 4 * TILE, VIDEO, 3))
    for ref, source, target, part in moves:
        scale, shift = 1.0 + mod_ref[part + 1 : part + 2, :], mod_ref[part : part + 1, :]
        for at in (0, 16):
            rows = ref[source + at : source + at + 16, :] * scale + shift
            input_out[pl.ds(pl.multiple_of(target + at, 16), 16), :] = rows.astype(jnp.bfloat16)
    for ref, place in zip(pieces[:7], places):
        for core in range(2):
            start = pl.multiple_of(core * 1536 + place * 192, 32)
            at = KEYS_AT + core * 192
            weight_ref[pl.ds(start, 192), :] = ref[at : at + 192, :]
    right_ref, left_ref, place = pieces[7], pieces[8], places[7]
    start = pl.multiple_of(place * 192, 32)
    weight_ref[pl.ds(start, 192), :] = right_ref[KEYS_AT : KEYS_AT + 192, :]
    start = pl.multiple_of(1536 + place * 192, 32)
    weight_ref[pl.ds(start, BLOCK), :] = right_ref[KEYS_AT + 192 :, :]
    start = pl.multiple_of(1536 + place * 192 + BLOCK, 32)
    weight_ref[pl.ds(start, BLOCK), :] = left_ref[:BLOCK, :]
    raw = matmul(input_out[...], weight_ref[...])
    lanes = lax.broadcasted_iota(jnp.int32, (1, 256), 1)
    key_raw = raw[:, :256]
    key = norm_and_rotate(
        key_raw,
        gain_ref[...],
        average_ref[...],
        partner_ref[...],
        cosine_ref[...],
        sine_ref[...],
    )
    keys_out[:, :256] = jnp.where(lanes < 192, key, key_raw).astype(jnp.bfloat16)
    keys_out[:, 256:] = raw[:, 256:384].astype(jnp.bfloat16)


def project_query(ids, input_ref, near_low, near_high, far_low, far_high, *refs):
    average_ref, partner_ref, cosine_ref, sine_ref, gain_ref, out, weight_ref = refs
    weight_ref[:, 192:] = jnp.zeros((WIDTH, 64), jnp.bfloat16)
    yh = ids[2]
    for ref, at in (
        (near_low, yh * BLOCK),
        (near_high, yh * BLOCK + HALF),
        (far_low, (1 - yh) * BLOCK),
        (far_high, (1 - yh) * BLOCK + HALF),
    ):
        for z in range(ZS):
            values = ref[z * HALF : z * HALF + HALF, :].astype(jnp.float32)
            for core in range(2):
                start = pl.multiple_of(core * 1536 + z * 192 + at, 16)
                weight_ref[pl.ds(start, HALF), :192] = values[
                    :, core * 192 : core * 192 + 192
                ].astype(jnp.bfloat16)
    raw = matmul(input_ref[:VIDEO, :], weight_ref[...])
    query = norm_and_rotate(
        raw,
        gain_ref[...],
        average_ref[...],
        partner_ref[...],
        cosine_ref[:VIDEO, :],
        sine_ref[:VIDEO, :],
    )
    out[...] = (query.astype(jnp.bfloat16).astype(jnp.float32) * 0.125).astype(jnp.bfloat16)


def rotary_tables(ids, rate_ref, cosine_ref, sine_ref):
    token = lax.broadcasted_iota(jnp.int32, (KEYS, 256), 0)
    lane = lax.broadcasted_iota(jnp.int32, (KEYS, 256), 1) % 64
    frame = token % 32 // 8
    height = 4 * ids[1] + token // 256 * 2 + token % 8 // 4
    across = token % 256 // 32 * 4 + token % 4
    place = jnp.where(lane < 16, frame, jnp.where(lane < 40, height, across))
    angle = jnp.where(token < VIDEO, place.astype(jnp.float32) * rate_ref[...], 0.0)
    back = jnp.logical_or(
        jnp.logical_and(lane >= 8, lane < 16),
        jnp.logical_or(jnp.logical_and(lane >= 28, lane < 40), lane >= 52),
    )
    cosine_ref[...] = jnp.cos(angle)
    sine = jnp.sin(angle)
    sine_ref[...] = jnp.where(back, sine, -sine)


def usable_bias(place_ref, count, first, z, limit):
    last = min(first + count, VIDEO)
    usable = place_ref[first:last, :] < limit - 128 * z
    bias = jnp.where(usable, 0.0, NEG_FILL).astype(jnp.bfloat16)
    if first + count > VIDEO:
        text_at = lax.broadcasted_iota(jnp.int32, (TEXT_PART, 128), 0)
        text_at += jnp.minimum(TEXT_PART * z, 226 - TEXT_PART)
        text = jnp.where(text_at >= TEXT_PART * z, 0.0, NEG_FILL).astype(jnp.bfloat16)
        bias = jnp.concatenate([bias, text], axis=0)
    return bias


def token_places():
    token = np.arange(VIDEO)
    height = token // 256 * 2 + token % 8 // 4
    place = (token % 32 // 8 * 32 + height) * 32 + token % 256 // 32 * 4 + token % 4
    return jnp.asarray(np.broadcast_to(place.astype(np.int32)[:, None], (VIDEO, 128)).copy())


def attend_pieces(ids, counts, place_ref, query_ref, pieces, old, new, finish):
    z, limit = ids[1], counts[ids[2]]
    loaded = []
    for ref, dz, first, count in pieces:
        values = ref[...]
        bias = usable_bias(place_ref, count, first, (z + dz + ZS) % ZS, limit)
        loaded.append((values, bias))
    values = jnp.concatenate([entry[0] for entry in loaded], axis=0)
    bias = jnp.concatenate([entry[1] for entry in loaded], axis=0)
    ones = jnp.ones(bias.shape, jnp.bfloat16)
    lanes = lax.broadcasted_iota(jnp.int32, (1, 128), 1)
    pick = jnp.where(lanes == 0, 1.0, 0.0).astype(jnp.bfloat16)
    keys = [jnp.concatenate([values[:, at : at + 128], bias], axis=1) for at in (0, 128)]
    mixes = [jnp.concatenate([values[:, at : at + 128], ones], axis=1) for at in (128, 256)]
    for start in range(0, VIDEO, QUERIES):
        rows = slice(start, start + QUERIES)
        finished = []
        for head in range(3):
            key_tile, mix_tile = (0, 0, 1)[head], (0, 1, 1)[head]
            inside = (lanes < 64) if head != 1 else (lanes >= 64)
            query = query_ref[rows, key_tile * 128 : key_tile * 128 + 128]
            query = jnp.where(inside, query, jnp.zeros_like(query))
            query = jnp.concatenate([query, jnp.broadcast_to(pick, query.shape)], axis=1)
            scores = matmul_nt(query, keys[key_tile])
            best = jnp.max(scores, axis=1, keepdims=True)
            if old is None:
                powers = jnp.exp(scores - best).astype(jnp.bfloat16)
                mixed = matmul(powers, mixes[mix_tile])
                gathered, total = mixed[:, :128], mixed[:, 128:]
                best = jnp.broadcast_to(best, gathered.shape)
            else:
                best_old = old[0][head, rows, :]
                best = jnp.maximum(best_old, best)
                powers = jnp.exp(scores - best[:, :1]).astype(jnp.bfloat16)
                mixed = matmul(powers, mixes[mix_tile])
                rescale = jnp.exp(best_old - best)
                total = old[1][head, rows, :] * rescale + mixed[:, 128:]
                gathered = old[2][head, rows, :] * rescale + mixed[:, :128]
            if finish is None:
                new[0][head, rows, :] = best
                new[1][head, rows, :] = total
                new[2][head, rows, :] = gathered
            else:
                finished.append(gathered / total)
        if finish is not None:
            finish[rows, :] = jnp.concatenate(
                [finished[0][:, 64:], finished[1][:, :64], finished[2][:, 64:]], axis=1
            ).astype(jnp.bfloat16)


def attend_first(ids, counts, place_ref, query_ref, own_ref, *new):
    attend_pieces(ids, counts, place_ref, query_ref, [(own_ref, 0, 0, KEYS)], None, new, None)


def attend_more(dz, ids, counts, place_ref, query_ref, right_ref, left_ref, *states):
    pieces = [(right_ref, -dz, 0, KEYS), (left_ref, dz, 0, KEYS)]
    attend_pieces(ids, counts, place_ref, query_ref, pieces, states[:3], states[3:], None)


def attend_last(
    ids, counts, place_ref, query_ref, right_ref, left_ref, best, total, gathered, out_ref
):
    half = KEYS // 2
    pieces = [(right_ref, -4, 0, half), (left_ref, 4, half, half)]
    attend_pieces(ids, counts, place_ref, query_ref, pieces, (best, total, gathered), None, out_ref)


def project_out(ids, own_ref, other_ref, weight_ref, mod_ref, out_ref):
    first = ids[0] == 0
    half = WIDTH // 2
    gate = mod_ref[2:3, pl.ds(pl.multiple_of(ids[0] * half, half), half)]
    weight = weight_ref[...]
    for row in range(2):
        rows = slice(row * STRIP, row * STRIP + STRIP)
        own, other = own_ref[rows, :].astype(jnp.float32), other_ref[rows, :].astype(jnp.float32)
        attended = jnp.concatenate(
            [jnp.where(first, own, other), jnp.where(first, other, own)], axis=1
        ).astype(jnp.bfloat16)
        gated = (matmul_nt(attended, weight) * gate).astype(jnp.bfloat16)
        for col in range(8):
            out_ref[row * 8 + col] = gated[col * TILE : col * TILE + TILE, :]


def sum_cols(ids, parts_ref, own_ref, other_ref):
    for ref, item in ((own_ref, ids[0]), (other_ref, 1 - ids[0])):
        total = parts_ref[item * 8].astype(jnp.float32)
        for peer in range(1, 8):
            total += parts_ref[item * 8 + peer].astype(jnp.float32)
        ref[...] = total.astype(ref.dtype)


def finish_rows(ids, hidden_ref, own_ref, other_ref, out_ref):
    first = ids[0] == 0
    half = WIDTH // 2
    own, other = own_ref[...], other_ref[...].astype(jnp.float32)
    low, high = jnp.where(first, own, other), jnp.where(first, other, own)
    out_ref[:, :half] = (hidden_ref[:, :half].astype(jnp.float32) + low).astype(jnp.bfloat16)
    out_ref[:, half:] = (hidden_ref[:, half:].astype(jnp.float32) + high).astype(jnp.bfloat16)


def rotary_rates():
    rates = []
    for band in (16, 24, 24):
        half = band // 2
        rate = np.exp(-math.log(10000.0) * (2.0 * np.arange(half) / band)).astype(np.float32)
        rates += [rate, rate]
    return jnp.asarray(np.tile(np.concatenate(rates), 4)[None, :])


def constant_matrices():
    average = np.zeros((256, 256), np.float32)
    partner = np.zeros((256, 256), np.float32)
    for head in range(4):
        average[head * 64 : head * 64 + 64, head * 64 : head * 64 + 64] = 1.0 / 64
        at = head * 64
        for band in (16, 24, 24):
            half = band // 2
            for entry in range(half):
                partner[at + half + entry, at + entry] = 1.0
                partner[at + entry, at + half + entry] = 1.0
            at += band
    return jnp.asarray(average, jnp.bfloat16), jnp.asarray(partner, jnp.bfloat16)


def on_device(
    hidden_video,
    hidden_text,
    step,
    valid_count,
    mod_weight,
    query_weight,
    key_weight,
    value_weight,
    out_weight,
    query_gain,
    key_gain,
):
    c = lax.axis_index("item")
    row = lax.axis_index("row")
    col = lax.axis_index("col")
    z, yh = row // 2, row % 2
    ids = jnp.stack([c, z, yh, col // 2, col % 2]).astype(jnp.int32)
    after = lax.optimization_barrier

    with jax.named_scope("start"):
        near_rows = call(stack_rows, shape((2 * BLOCK, 384)), key_weight, value_weight, smem=0)
        far_rows = send(near_rows, dyh=1)
        home_tile = hidden_video.reshape(TILE, WIDTH)
        tile = trade_items(home_tile)
        active = jax.nn.silu(time_features(step, 512)).astype(jnp.bfloat16)
        slots = call(
            own_modulation,
            shape((32, 8, 128), jnp.float32),
            active,
            jnp.transpose(mod_weight, (0, 2, 1)),
            scratch=[pltpu.VMEM((16, 128), jnp.float32)],
            smem=0,
        )
        groups = [
            [core * 128 + 16 * z_at + peer for core in range(2) for peer in range(16)]
            for z_at in range(ZS)
        ]
        slots = lax.all_to_all(slots, AXES, 0, 0, tiled=True, axis_index_groups=groups)
        far_rows, slots, tile, ids = after((far_rows, slots, tile, ids))

    with jax.named_scope("block"):
        other = call(
            split_weights, shape((3 * BLOCK, 384)), ids, near_rows, far_rows, query_weight
        )
        next_tile = send(tile, dyl=1)
        block = call(
            join_weights,
            shape((BLOCK_ROWS, 384)),
            ids,
            near_rows,
            far_rows,
            send(other, dc=1),
            query_weight,
            out_weight,
            slots,
        )
        block, tile = after((block, tile))

    with jax.named_scope("ring1"):
        right, left = send(block, dz=1), send(block, dz=-1)
        near = call(stack_rows, shape((2 * TILE, WIDTH)), tile, next_tile, smem=0)
        near_right, near_left = send(near, dx=1), send(near, dx=-1)
        text = lax.dynamic_slice_in_dim(
            hidden_text[0], jnp.minimum(TEXT_PART * z, 226 - TEXT_PART), TEXT_PART, 0
        )
        right, left, near_right, near_left, text = after(
            (right, left, near_right, near_left, text)
        )
    pieces = [block, right, left]

    with jax.named_scope("ring2"):
        right, left = send(right, dz=1), send(left, dz=-1)
        far_right, far_left = send(near_right[:TILE], dx=1), send(near_left[TILE:], dx=-1)
        text_other = send(text, dc=1)
        other_near = send(near, dc=1)
        right, left, far_right, far_left, text_other, other_near = after(
            (right, left, far_right, far_left, text_other, other_near)
        )
    pieces += [right, left]

    with jax.named_scope("ring3"):
        right, left = send(right, dz=1), send(left, dz=-1)
        other_right, other_left = send(near_right, dc=1), send(near_left, dc=1)
        far_right_other, far_left_other = send(far_right, dc=1), send(far_left, dc=1)
        first = call(
            norm_tokens, shape((4 * TILE, WIDTH), jnp.float32), near, other_near, smem=0
        )
        text = jnp.where(c == yh, text, text_other)
        average, partner = constant_matrices()
        cosine, sine = call(
            rotary_tables, [shape((KEYS, 256), jnp.float32)] * 2, ids, rotary_rates()
        )
        tables = (average, partner, cosine, sine)
        others = (other_right, other_left, far_right_other, far_left_other)
        right, left, others, text, first, tables = after(
            (right, left, others, text, first, tables)
        )
        other_right, other_left, far_right_other, far_left_other = others
    pieces += [right, left]

    with jax.named_scope("ring4"):
        right = send(right[:CUT], dz=1)
        left = send(left[CUT:], dz=-1)
        second = call(
            norm_tokens,
            shape((8 * TILE, WIDTH), jnp.float32),
            near_right,
            near_left,
            other_right,
            other_left,
            smem=0,
        )
        third = call(
            norm_tokens,
            shape((5 * TILE, WIDTH), jnp.float32),
            far_right,
            far_left,
            far_right_other,
            far_left_other,
            text,
            smem=0,
        )
        right, left, second, third = after((right, left, second, third))

    with jax.named_scope("projections"):
        keys, inputs, query_low, query_high, out_near, modulation = call(
            project_keys,
            [
                shape((KEYS, 384)),
                shape((KEYS, WIDTH)),
                shape((ZS * HALF, 384)),
                shape((ZS * HALF, 384)),
                shape((ZS * BLOCK, 384)),
                shape((8, WIDTH), jnp.float32),
            ],
            ids,
            first,
            second,
            third,
            *pieces,
            right,
            left,
            *tables,
            key_gain[None, :],
            scratch=[pltpu.VMEM((WIDTH, 384), jnp.bfloat16), pltpu.VMEM((ZS, 8, 384), jnp.float32)],
            flops=2 * KEYS * WIDTH * 384,
            room=32,
        )

    with jax.named_scope("attention"):
        state_shapes = [shape((3, VIDEO, 128), jnp.float32)] * 3
        cost = 4 * VIDEO * KEYS * 256 * 3
        rights, lefts = [], []
        places = token_places()

        def more(away, state):
            def body(*refs):
                attend_more(away, *refs)

            args = (ids, valid_count, places, query, rights[away - 1], lefts[away - 1], *state)
            return call(body, state_shapes, *args, smem=2, flops=2 * cost)

        right, left = send(keys, dz=1), send(keys, dz=-1)
        far_low, far_high = send(query_low, dyh=1), send(query_high, dyh=1)
        right, left, out_near = after((right, left, out_near))
        rights.append(right)
        lefts.append(left)

        right, left = send(right, dz=1), send(left, dz=-1)
        out_far = send(out_near, dyh=1)
        query = call(
            project_query,
            shape((VIDEO, 256)),
            ids,
            inputs,
            query_low,
            query_high,
            far_low,
            far_high,
            *tables,
            query_gain[None, :],
            scratch=[pltpu.VMEM((WIDTH, 256), jnp.bfloat16)],
            flops=2 * VIDEO * WIDTH * 256,
            room=24,
        )
        state = call(
            attend_first, state_shapes, ids, valid_count, places, query, keys, smem=2, flops=cost
        )
        right, left, *state = after((right, left, *state))
        rights.append(right)
        lefts.append(left)

        right, left = send(right, dz=1), send(left, dz=-1)
        state = more(2, more(1, state))
        right, left, *state = after((right, left, *state))
        rights.append(right)
        lefts.append(left)

        right, left = send(right[: KEYS // 2], dz=1), send(left[KEYS // 2 :], dz=-1)
        state = more(3, state)
        last_weight = call(sort_out, shape((WIDTH // 2, 384)), ids, out_near, out_far)
        right, left, last_weight, *state = after((right, left, last_weight, *state))
        attended = call(
            attend_last,
            shape((VIDEO, 192)),
            ids,
            valid_count,
            places,
            query,
            right,
            left,
            *state,
            smem=2,
            flops=cost,
        )

    with jax.named_scope("output"):
        parts = call(
            project_out,
            shape((16, TILE, WIDTH // 2)),
            ids,
            attended,
            send(attended, dc=1),
            last_weight,
            modulation,
        )
        groups = [[16 * z_at + peer for peer in range(16)] for z_at in range(ZS)]
        parts = lax.all_to_all(
            parts, ("row", "col"), 0, 0, tiled=True, axis_index_groups=groups
        )
        own_sum, other_sum = call(
            sum_cols,
            [shape((TILE, WIDTH // 2), jnp.float32), shape((TILE, WIDTH // 2))],
            ids,
            parts,
        )
        result = call(
            finish_rows,
            shape((TILE, WIDTH)),
            ids,
            home_tile,
            own_sum,
            send(other_sum, dc=1),
        )
        return result.reshape(hidden_video.shape)


def solution(mesh):
    placed = (
        P("item", None, "row", "col", None),
        P("item", None, None),
        P(),
        P(),
        P(None, None, ("item", "row", "col")),
        P(("item", "row"), "col"),
        P(("item", "row"), "col"),
        P(("item", "row"), "col"),
        P(("item", "row"), "col"),
        P(),
        P(),
    )
    return jax.shard_map(
        on_device,
        mesh=mesh,
        in_specs=placed,
        out_specs=P("item", None, "row", "col", None),
        check_vma=False,
    )
```
